256 devices in a mesh: group: 8 (over x_hi, y), fsdp: 32 (over z, x_lo, core).
Axes of the slice: x: 4 (x_hi: 2, x_lo: 2; x = x_hi * 2 + x_lo), y: 4, z: 8, core: 2. Of those that a mesh axis runs over, the one named last changes fastest.
Arguments:
- tokens: bfloat16 [131072, 8192], P(('group', 'fsdp')), may hold values from -6 to 6
- target: bfloat16 [131072, 512], P(('group', 'fsdp')), may hold values from -6 to 6
- weight: bfloat16 [8192, 512], P('fsdp'), may hold values from -6 to 6
- momentum: float32 [8192, 512], P('fsdp', 'group'), may hold values from -4 to 4
Outputs:
- new_weight: bfloat16 [8192, 512], P('fsdp')
- new_momentum: float32 [8192, 512], P('fsdp', 'group')
The draws below stay inside these ranges and needn't reach their ends.
All inputs are finite; a program needn't handle non-finite values.
Results may differ from the reference program's by a relative error of at most 0.0055.
Values may be sent and summed in bfloat16 or wider, within the bound.
A program may use at most 128 MiB of HBM per device.

```python
import math
import jax
import jax.numpy as jnp
from jax import lax

D = 8192
KVW = 512
BLOCK = 32
TOK_DEV = 512
TOKENS = 131072
N_GROUP = 8
N_FSDP = 32


def level_of(own_key, shape, shards, least, top_value):
    gain, own = 1.0, jax.random.fold_in(own_key, 6)
    for axis_at, blocks in shards:
        heights = jnp.exp(jax.random.uniform(jax.random.fold_in(own, axis_at), (blocks,), jnp.float32, least / len(shards), top_value / len(shards)))
        gain = gain * jnp.repeat(heights, shape[axis_at] // blocks).reshape([-1 if axis == axis_at else 1 for axis in range(len(shape))])
    return gain


def centred(key, dims, scale, limit, shards=(), dtype=jnp.bfloat16):
    result = jax.random.normal(key, dims, jnp.float32) * scale
    if len(shards) > 0:
        result = level_of(key, dims, shards, -0.22, 0.18) * result
    return jnp.clip(result, min=-limit, max=limit).astype(dtype)


def setup_inputs(seed: int = 0) -> dict:
    splits = jax.random.split(jax.random.key(seed), 5)
    return {
        "tokens": centred(splits[0], (TOKENS, D), 1.0, 6.0, ((0, 256),)),
        "target": centred(splits[1], (TOKENS, KVW), 1.0, 6.0, ((0, 256),)),
        "weight": centred(splits[2], (D, KVW), 1.0, 6.0, ((0, 32),)),
        "momentum": centred(splits[3], (D, KVW), 0.5, 4.0, ((0, 32), (1, 8)), jnp.float32),
    }


inner_rate = 0.5
momentum_decay = 0.9
outer_rate = 0.7

def encode(delta):
    row_count, width_all = delta.shape
    blocked = delta.reshape(row_count, width_all // BLOCK, BLOCK)
    largest = lax.optimization_barrier(jnp.max(jnp.abs(blocked), axis=2))
    block_scale = jnp.exp2(jnp.ceil(jnp.log2(largest / 6.0 + 1e-30))).astype(jnp.bfloat16)
    scale_wide = block_scale.astype(jnp.float32)[:, :, None]
    code_vals = jnp.clip(blocked / scale_wide, -6.0, 6.0).astype(jnp.bfloat16)
    return (code_vals, block_scale)

def reference(tokens, target, weight, momentum):
    group_tokens = TOK_DEV * N_FSDP
    root_width = math.sqrt(D)
    grad_scale = math.sqrt(D / group_tokens)
    token_blocks = tokens.reshape(N_GROUP, group_tokens, D)
    target_blocks = target.reshape(N_GROUP, group_tokens, KVW)

    def one_group(running, items):
        features, wanted = items
        values = jnp.dot(features, weight, preferred_element_type=jnp.float32) / root_width
        cotangent = ((values - wanted.astype(jnp.float32)) * grad_scale).astype(jnp.bfloat16)
        gradient = lax.dot_general(features, cotangent, (((0,), (0,)), ((), ())), preferred_element_type=jnp.float32) / root_width
        code_vals, block_scale = encode(inner_rate * gradient)
        code_vals, block_scale = lax.optimization_barrier((code_vals, block_scale))
        decoded = code_vals.astype(jnp.float32) * block_scale.astype(jnp.float32)[:, :, None]
        return (running + decoded.reshape(D, KVW), None)
    summed, _ = lax.scan(one_group, jnp.zeros((D, KVW), jnp.float32), (token_blocks, target_blocks))
    average = summed / N_GROUP
    new_momentum = momentum_decay * momentum + average
    new_weight = (weight.astype(jnp.float32) - outer_rate * (average + momentum_decay * new_momentum)).astype(jnp.bfloat16)
    return (new_weight, new_momentum)
```

```python
import functools
import math

import jax
import jax.numpy as jnp
from jax import lax
from jax.experimental import pallas as pl
from jax.experimental.pallas import tpu as pltpu
from jax.sharding import PartitionSpec as P

BLOCK = 32
inner_rate = 0.5
momentum_decay = 0.9
outer_rate = 0.7

MESH = pl.DeviceIdType.MESH
F32 = jnp.float32
BF16 = jnp.bfloat16

NZ, NX, NC, NY, NH = 8, 2, 2, 4, 2
NG = NY * NH
D, KVW, TOK = 8192, 512, 512
ROWS = D // (NZ * NX * NC)
HALF = ROWS // 2
QUART = ROWS // 4
OWN = KVW // NG
LANES = 128

GATHER = (
    (0, 0), (0, 1), (1, 0), (-1, 0), (1, 1), (-1, 1), (2, 0), (-2, 0),
    (2, 1), (-2, 1), (3, 0), (-3, 0), (3, 1), (-3, 1), (4, 0), (4, 1),
)
INDEX = {o: k for k, o in enumerate(GATHER)}
N = len(GATHER)
SCATTER = (
    (4, 1), (4, 0), (3, 1), (-3, 1), (3, 0), (-3, 0), (1, 1), (-1, 1),
    (0, 1), (2, 1), (-2, 1), (2, 0), (-2, 0), (1, 0), (-1, 0), (0, 0),
)
LAG_FINAL, LAG_CORE = 3, 1


def children(o, s):
    oz, ox = o
    out = []
    if oz == 4:
        return out
    if ox == 0:
        if 0 <= oz < 3 or (oz == 3 and s == 0):
            out.append(("up", (oz + 1, 0)))
        if -3 < oz <= 0 or (oz == -3 and s == 1):
            out.append(("down", (oz - 1 if oz > -3 else 4, 0)))
        if abs(oz) <= 2:
            out.append(("across", (oz, 1)))
    else:
        if oz == 2 or (oz == 3 and s == 0):
            out.append(("up", (oz + 1, 1)))
        if oz == -2 or (oz == -3 and s == 1):
            out.append(("down", (oz - 1 if oz > -3 else 4, 1)))
    return out


REVERSE = {"up": "down", "down": "up", "across": "across"}
PARENT = {(c, s): (REVERSE[d], o) for o in GATHER for s in range(2) for d, c in children(o, s)}


def pick(k, table):
    got = jnp.int32(table[0])
    for at in range(1, len(table)):
        got = jnp.where(k == at, jnp.int32(table[at]), got)
    return got


def kernel(
    tok_hbm, tgt_hbm, w_hbm, mom_hbm, nw_hbm, nm_hbm,
    x_own, x_oth, wfull, acc, tgt, mom, cot_own, cot_par, gbuf, sbuf, rbuf,
    dec, gsum, w_t, m_t, upd, wn_t, nw, nm,
    load_sem, out_sem, send_sem, zx_sem, fin_sem, core_sem, tok_sem, cot_sem, rs_sem, ex_sem, up_sem,
):
    g = lax.axis_index("group")
    f = lax.axis_index("fsdp")
    xh, y = g // NY, g % NY
    z, xl, c = f // (NX * NC), (f // NC) % NX, f % NC

    def at(zz, xx, cc):
        return (zz * NX + xx) * NC + cc

    to = {
        "up": {"group": g, "fsdp": at((z + 1) % NZ, xl, c)},
        "down": {"group": g, "fsdp": at((z + NZ - 1) % NZ, xl, c)},
        "across": {"group": g, "fsdp": at(z, 1 - xl, c)},
        "core": {"group": g, "fsdp": at(z, xl, 1 - c)},
        "y_up": {"group": xh * NY + (y + 1) % NY, "fsdp": f},
        "y_down": {"group": xh * NY + (y + NY - 1) % NY, "fsdp": f},
        "beyond": {"group": (1 - xh) * NY + y, "fsdp": at(z, 1 - xl, c)},
    }

    def send(src, dst, s_sem, r_sem, device):
        copy = pltpu.make_async_remote_copy(
            src_ref=src, dst_ref=dst, send_sem=s_sem, recv_sem=r_sem, device_id=device, device_id_type=MESH
        )
        copy.start()

    def wait(ref, sem):
        pltpu.make_async_copy(ref, ref, sem).wait()

    def chip_of(enc):
        return (z + NZ - enc // 2) % NZ, (xl + enc) % 2

    def shard_of(o):
        zz, xx = chip_of((o[0] % NZ) * 2 + o[1])
        return at(zz, xx, c)

    w_load = pltpu.make_async_copy(w_hbm, wfull.at[pl.ds(pl.multiple_of(f * ROWS, ROWS), ROWS)], load_sem.at[0])
    w_load.start()

    @pl.loop(0, NZ * NX * NC)
    def _(j):
        pltpu.make_async_copy(
            tok_hbm.at[:, pl.ds(pl.multiple_of(j * ROWS, ROWS), ROWS)], x_own.at[j], load_sem.at[1]
        ).start()

    t_load = pltpu.make_async_copy(tgt_hbm, tgt, load_sem.at[2])
    t_load.start()
    m_load = pltpu.make_async_copy(mom_hbm, mom, load_sem.at[3])
    m_load.start()

    barrier = pltpu.get_barrier_semaphore()
    for name in ("up", "down", "across", "core", "beyond"):
        pl.semaphore_signal(barrier, inc=1, device_id=to[name], device_id_type=MESH)
    for step in range(1, NG):
        pl.semaphore_signal(
            barrier, inc=1, device_id={"group": (g + step) % NG, "fsdp": f}, device_id_type=MESH
        )
    pl.semaphore_wait(barrier, 5 + NG - 1)
    w_load.wait()

    mine = pl.multiple_of(((y + xh) % 2) * HALF, HALF)
    theirs = pl.multiple_of(HALF - mine, HALF)

    def rows(shard, start, count):
        return wfull.at[pl.ds(pl.multiple_of(shard * ROWS + start, 16), count)]

    def pass_on(k):
        o = GATHER[k]
        shard = shard_of(o)
        for s in range(2):
            piece = rows(shard, mine + s * QUART, QUART)
            if k > 0:
                wait(piece, zx_sem.at[k, s])
            for direction, child in children(o, s):
                send(piece, piece, send_sem.at[0], zx_sem.at[INDEX[child], s], to[direction])
        if k > 0:
            for name, start, count in (("y_up", 0, 48), ("y_down", 48, 48)):
                piece = rows(shard, mine + start, count)
                send(piece, piece, send_sem.at[0], fin_sem.at[k], to[name])
        if o != (0, 1):
            piece = rows(shard, mine + 96, 32)
            send(piece, piece, send_sem.at[0], fin_sem.at[INDEX[(o[0], 1 - o[1])]], to["beyond"])

    enc_table = [(oz % NZ) * 2 + ox for oz, ox in GATHER]
    acc[...] = jnp.zeros_like(acc)

    @pl.loop(0, N + LAG_FINAL + LAG_CORE)
    def _(t):
        for k in range(N):
            @pl.when(t == k)
            def _(k=k):
                pass_on(k)

        @pl.when(t < N)
        def _():
            shard = t * NC + 1 - c
            send(
                tok_hbm.at[:, pl.ds(pl.multiple_of(shard * ROWS, ROWS), ROWS)],
                x_oth.at[t], send_sem.at[1], tok_sem.at[0], to["core"],
            )

        @pl.when((t >= LAG_FINAL) & (t < N + LAG_FINAL))
        def _():
            k = t - LAG_FINAL
            zz, xx = chip_of(pick(k, enc_table))
            shard = at(zz, xx, c)

            @pl.when(k > 0)
            def _():
                wait(rows(shard, theirs, HALF), fin_sem.at[k])

            piece = rows(shard, 0, ROWS)
            send(piece, piece, send_sem.at[0], core_sem.at[k], to["core"])

        @pl.when(t == LAG_FINAL)
        def _():
            wait(x_own, load_sem.at[1])

        @pl.when(t >= LAG_FINAL + LAG_CORE)
        def _():
            k = t - LAG_FINAL - LAG_CORE
            zz, xx = chip_of(pick(k, enc_table))
            a, b = at(zz, xx, c), at(zz, xx, 1 - c)
            wait(rows(b, 0, ROWS), core_sem.at[k])
            acc[...] += jnp.dot(
                x_own[a], wfull[pl.ds(pl.multiple_of(a * ROWS, ROWS), ROWS), :], preferred_element_type=F32
            ) + jnp.dot(
                x_own[b], wfull[pl.ds(pl.multiple_of(b * ROWS, ROWS), ROWS), :], preferred_element_type=F32
            )

    root_width = math.sqrt(D)
    grad_scale = math.sqrt(D / (TOK * NZ * NX * NC))
    t_load.wait()
    cot = (acc[...] / root_width - tgt[...].astype(F32)) * grad_scale
    cot_own[...] = cot.T.astype(BF16)
    send(cot_own, cot_par, send_sem.at[2], cot_sem.at[0], to["core"])

    m_load.wait()
    w_t[...] = wfull[pl.ds(pl.multiple_of(f * ROWS, ROWS), ROWS), :].astype(F32).T
    m_t[...] = jnp.concatenate([mom[...], jnp.zeros_like(mom)], axis=1).T[:OWN]

    wait(x_oth, tok_sem.at[0])
    wait(cot_par, cot_sem.at[0])

    def leaf(o, s):
        return not children(o, s)

    def send_sum(o, s):
        k = INDEX[o]
        direction, _ = PARENT[o, s]
        send(sbuf.at[k, s], rbuf.at[k, s], send_sem.at[3], rs_sem.at[k, s], to[direction])

    scatter_enc = [(oz % NZ) * 2 + ox for oz, ox in SCATTER]
    scatter_k = [INDEX[o] for o in SCATTER]

    @pl.loop(0, N)
    def _(t):
        zz, xx = chip_of(pick(t, scatter_enc))
        k = pick(t, scatter_k)
        grad = jnp.dot(cot_own[...], x_own[at(zz, xx, c)], preferred_element_type=F32) + jnp.dot(
            cot_par[...], x_oth[zz * NX + xx], preferred_element_type=F32
        )
        for s in range(2):
            gbuf[k, s] = grad[:, s * LANES : (s + 1) * LANES]
            sbuf[k, s] = grad[:, s * LANES : (s + 1) * LANES].astype(BF16)
        for n, o in enumerate(SCATTER):
            if any(leaf(o, s) for s in range(2)):
                @pl.when(t == n)
                def _(o=o):
                    for s in range(2):
                        if leaf(o, s):
                            send_sum(o, s)

    def total(o, s):
        k = INDEX[o]
        got = gbuf[k, s]
        for _, child in children(o, s):
            kc = INDEX[child]
            wait(rbuf.at[kc, s], rs_sem.at[kc, s])
            got = got + rbuf[kc, s].astype(F32)
        return got

    steps = (
        ((3, 1), 0), ((-3, 1), 1), ((2, 1), 1), ((-2, 1), 0), ((3, 0), 0), ((-3, 0), 1),
        ((2, 1), 0), ((-2, 1), 1), ((2, 0), 1), ((-2, 0), 0), ((1, 0), 1), ((-1, 0), 0),
        ((2, 0), 0), ((-2, 0), 1), ((1, 0), 0), ((-1, 0), 1),
    )
    for o, s in steps:
        sbuf[INDEX[o], s] = total(o, s).astype(BF16)
        send_sum(o, s)

    mine_rows = pl.multiple_of(g * OWN, OWN)
    for s in (1, 0):
        delta = (inner_rate * (total((0, 0), s) / root_width)).reshape(KVW // BLOCK, BLOCK, LANES)
        largest = jnp.max(jnp.abs(delta), axis=1, keepdims=True)
        block_scale = jnp.exp2(jnp.ceil(jnp.log2(largest / 6.0 + 1e-30))).astype(BF16).astype(F32)
        code = jnp.clip(delta / block_scale, -6.0, 6.0).astype(BF16)
        dec[s] = (code.astype(F32) * block_scale).reshape(KVW, LANES).astype(BF16)
        for step in range(1, NG):
            other = (g + step) % NG
            send(
                dec.at[s, pl.ds(pl.multiple_of(other * OWN, OWN), OWN)], gsum.at[s, g],
                send_sem.at[4], ex_sem.at[s], {"group": other, "fsdp": f},
            )
        gsum[s, g] = dec[s, pl.ds(mine_rows, OWN), :]

    for s in (1, 0):
        wait(gsum.at[s, pl.ds(0, NG - 1)], ex_sem.at[s])
        summed = gsum[s, 0].astype(F32)
        for step in range(1, NG):
            summed = summed + gsum[s, step].astype(F32)
        average = summed / NG
        lanes = slice(s * LANES, (s + 1) * LANES)
        new_mom = momentum_decay * m_t[:, lanes] + average
        own_w = w_t[pl.ds(mine_rows, OWN), lanes]
        new_w = (own_w - outer_rate * (average + momentum_decay * new_mom)).astype(BF16)
        upd[s] = new_w
        for step in range(1, NG):
            other = (g + step) % NG
            send(
                upd.at[s], wn_t.at[s, pl.ds(mine_rows, OWN)], send_sem.at[5], up_sem.at[s],
                {"group": other, "fsdp": f},
            )
        wn_t[s, pl.ds(mine_rows, OWN), :] = new_w
        nm[s * LANES : (s + 1) * LANES, :] = jnp.concatenate([new_mom, jnp.zeros_like(new_mom)], axis=0).T[:, :OWN]
    nm_out = pltpu.make_async_copy(nm, nm_hbm, out_sem.at[0])
    nm_out.start()

    for s in (1, 0):
        wait(wn_t.at[s, pl.ds(0, KVW - OWN)], up_sem.at[s])
        nw[s * LANES : (s + 1) * LANES, :] = wn_t[s].astype(F32).T.astype(BF16)
    nw_out = pltpu.make_async_copy(nw, nw_hbm, out_sem.at[1])
    nw_out.start()

    wait(wfull.at[pl.ds(0, (N - 1) * ROWS + N * ROWS)], send_sem.at[0])
    wait(x_oth, send_sem.at[1])
    wait(cot_own, send_sem.at[2])
    wait(sbuf.at[pl.ds(0, N - 1)], send_sem.at[3])
    wait(gsum.at[:, pl.ds(0, NG - 1)], send_sem.at[4])
    wait(gsum.at[:, pl.ds(0, NG - 1)], send_sem.at[5])
    nm_out.wait()
    nw_out.wait()


def body(tokens, target, weight, momentum):
    hbm = pl.BlockSpec(memory_space=pl.ANY)
    dma = pltpu.SemaphoreType.DMA
    return pl.pallas_call(
        kernel,
        out_shape=(
            jax.ShapeDtypeStruct((ROWS, KVW), BF16),
            jax.ShapeDtypeStruct((ROWS, OWN), F32),
        ),
        in_specs=[hbm] * 4,
        out_specs=(hbm, hbm),
        scratch_shapes=[
            pltpu.VMEM((NZ * NX * NC, TOK, ROWS), BF16),
            pltpu.VMEM((NZ * NX, TOK, ROWS), BF16),
            pltpu.VMEM((D, KVW), BF16),
            pltpu.VMEM((TOK, KVW), F32),
            pltpu.VMEM((TOK, KVW), BF16),
            pltpu.VMEM((ROWS, OWN), F32),
            pltpu.VMEM((KVW, TOK), BF16),
            pltpu.VMEM((KVW, TOK), BF16),
            pltpu.VMEM((N, 2, KVW, LANES), F32),
            pltpu.VMEM((N, 2, KVW, LANES), BF16),
            pltpu.VMEM((N, 2, KVW, LANES), BF16),
            pltpu.VMEM((2, KVW, LANES), BF16),
            pltpu.VMEM((2, NG, OWN, LANES), BF16),
            pltpu.VMEM((KVW, ROWS), F32),
            pltpu.VMEM((OWN, ROWS), F32),
            pltpu.VMEM((2, OWN, LANES), BF16),
            pltpu.VMEM((2, KVW, LANES), BF16),
            pltpu.VMEM((ROWS, KVW), BF16),
            pltpu.VMEM((ROWS, OWN), F32),
            dma((4,)), dma((2,)), dma((6,)), dma((N, 2)), dma((N,)), dma((N,)), dma((1,)), dma((1,)),
            dma((N, 2)), dma((2,)), dma((2,)),
        ],
        compiler_params=pltpu.CompilerParams(
            collective_id=0, has_side_effects=True, vmem_limit_bytes=56 * 1024 * 1024
        ),
        cost_estimate=pl.CostEstimate(
            flops=4 * TOK * D * KVW, bytes_accessed=2 * TOK * D + 4 * ROWS * KVW, transcendentals=0
        ),
    )(tokens, target, weight, momentum)


def solution(mesh):
    placed = (
        P(("group", "fsdp"), None),
        P(("group", "fsdp"), None),
        P("fsdp", None),
        P("fsdp", "group"),
    )
    return jax.shard_map(
        body,
        mesh=mesh,
        in_specs=placed,
        out_specs=(P("fsdp", None), P("fsdp", "group")),
        check_vma=False,
    )
```

```python
import math

import jax
import jax.numpy as jnp
from jax import lax
from jax.experimental import pallas as pl
from jax.experimental.pallas import tpu as pltpu
from jax.sharding import PartitionSpec as P

BLOCK = 32
inner_rate = 0.5
momentum_decay = 0.9
outer_rate = 0.7

MESH = pl.DeviceIdType.MESH
F32 = jnp.float32
BF16 = jnp.bfloat16

NZ, NX, NC, NY, NH = 8, 2, 2, 4, 2
NG = NY * NH
D, KVW, TOK = 8192, 512, 512
ROWS = D // (NZ * NX * NC)
HALF = ROWS // 2
OWN = KVW // NG
LANES = 128
QG, QR = 2, 2
PIECE = HALF // 2 // QG
PART = KVW // QR

GATHER_ACROSS = (-3, -2, 0, 1, 2)
SPLITS = (((32, 16, 16), (16, 32, 16)), ((32, 16, 16), (16, 16, 32)), ((16, 32, 16), (16, 16, 32)))
SPLIT_AT = (2, 1, 2, 0, 0, 1, 2, 0)
GATHER = (
    ("s", -1, 0, 1, 0), ("s", -1, 0, 1, 1), ("s", 1, 0, 0, 0), ("s", 1, 0, 0, 1), ("s", 1, 0, 1, 0),
    ("s", 0, 1, 0, 0), ("f", 0, 0, 0), ("f", 0, 0, 1), ("s", 0, 1, 0, 1), ("s", 0, 1, 1, 0), ("s", -1, 0, 0, 0),
    ("c", 0, 0), ("s", -1, 0, 0, 1), ("s", 1, 0, 1, 1), ("s", 0, 1, 1, 1), ("s", -2, 0, 1, 0), ("s", -1, 1, 1, 0),
    ("s", 2, 0, 0, 0), ("s", 1, 1, 0, 0), ("s", -1, 1, 0, 0), ("s", -2, 0, 1, 1), ("f", -1, 0, 1),
    ("s", 2, 0, 0, 1), ("f", 1, 0, 0), ("s", 1, 1, 0, 1), ("s", -1, 1, 0, 1), ("f", 0, 1, 0), ("s", -1, 1, 1, 1),
    ("s", -2, 0, 0, 0), ("s", 2, 0, 1, 0), ("s", 1, 1, 1, 0), ("f", -1, 0, 0), ("s", 2, 0, 1, 1), ("f", 1, 0, 1),
    ("s", -2, 0, 0, 1), ("s", 1, 1, 1, 1), ("f", 0, 1, 1), ("s", -2, 1, 1, 0), ("s", -3, 0, 1, 0),
    ("s", 2, 1, 0, 0), ("s", 3, 0, 0, 0), ("s", 2, 1, 0, 1), ("f", 2, 0, 0), ("s", 3, 0, 0, 1), ("f", -2, 0, 1),
    ("s", -2, 1, 1, 1), ("s", -3, 0, 1, 1), ("s", 3, 0, 1, 0), ("s", 2, 1, 1, 0), ("f", 1, 1, 0), ("f", -1, 1, 0),
    ("f", -1, 1, 1), ("d", 0, 0), ("s", -3, 1, 1, 0), ("s", 3, 0, 1, 1), ("f", 2, 0, 1), ("f", -2, 0, 0),
    ("f", 1, 1, 1), ("s", 2, 1, 1, 1), ("s", -3, 0, 0, 0), ("s", -3, 0, 0, 1), ("s", -2, 1, 0, 0),
    ("s", 4, 0, 1, 0), ("s", -2, 1, 0, 1), ("s", 3, 1, 0, 0), ("s", 4, 0, 0, 0), ("c", 0, 1), ("f", 2, 1, 0),
    ("s", 3, 1, 0, 1), ("f", -3, 0, 1), ("f", 3, 0, 0), ("s", 4, 0, 0, 1), ("s", 4, 0, 1, 1), ("f", -2, 1, 1),
    ("s", -3, 1, 1, 1), ("s", 3, 1, 1, 0), ("d", 0, 1), ("s", 4, 1, 1, 0), ("c", -1, 1), ("f", 3, 0, 1),
    ("c", -1, 0), ("s", 3, 1, 1, 1), ("s", -3, 1, 0, 0), ("f", 2, 1, 1), ("s", 4, 1, 0, 0), ("c", 1, 1),
    ("s", -3, 1, 0, 1), ("f", -3, 0, 0), ("d", -1, 1), ("f", -2, 1, 0), ("c", 1, 0), ("s", 4, 1, 0, 1),
    ("f", 3, 1, 0), ("d", -1, 0), ("f", 4, 0, 1), ("s", 4, 1, 1, 1), ("f", 4, 0, 0), ("f", 3, 1, 1),
    ("f", -3, 1, 1), ("c", 2, 1), ("d", 1, 0), ("d", 1, 1), ("f", -3, 1, 0), ("f", 4, 1, 0), ("c", -2, 1),
    ("c", 2, 0), ("d", 2, 1), ("f", 4, 1, 1), ("c", -2, 0), ("d", -2, 1), ("c", 3, 0), ("d", 2, 0), ("c", 3, 1),
    ("d", -2, 0), ("c", -3, 1), ("c", -3, 0), ("d", 3, 0), ("c", 4, 1), ("d", 3, 1), ("c", 4, 0), ("d", -3, 1),
    ("d", -3, 0), ("d", 4, 1), ("d", 4, 0),
)

SUM_ACROSS = (-2, -1, 0, 1, 2)
SUM = (
    ("u", 1, 1), ("p", 1, 1, 0, 0), ("p", 1, 1, 0, 1), ("u", 4, 1), ("p", 4, 1, 0, 0), ("p", 4, 1, 1, 0),
    ("p", 4, 1, 0, 1), ("p", 4, 1, 1, 1), ("u", 2, 0), ("u", -1, 0), ("p", 1, 1, 1, 0), ("u", 3, 1),
    ("p", 3, 1, 1, 0), ("u", -3, 1), ("p", -3, 1, 0, 0), ("u", -2, 1), ("p", 1, 1, 1, 1), ("u", 4, 0),
    ("p", 4, 0, 0, 0), ("p", 4, 0, 1, 0), ("u", -1, 1), ("u", 1, 0), ("p", -1, 1, 0, 0), ("u", -3, 0),
    ("p", 3, 1, 0, 0), ("p", -3, 1, 1, 0), ("u", 0, 0), ("p", -1, 1, 1, 0), ("u", 2, 1), ("u", 0, 1),
    ("p", 3, 1, 0, 1), ("p", -3, 1, 1, 1), ("u", 3, 0), ("p", 2, 1, 1, 0), ("u", -2, 0), ("p", 4, 0, 0, 1),
    ("p", 4, 0, 1, 1), ("p", -2, 1, 0, 0), ("p", 3, 1, 1, 1), ("p", -3, 0, 1, 0), ("p", -2, 1, 1, 0),
    ("p", 3, 0, 1, 0), ("p", -3, 0, 0, 0), ("p", -2, 1, 1, 1), ("p", 3, 0, 1, 1), ("p", -3, 1, 0, 1),
    ("p", 2, 1, 0, 0), ("p", 3, 0, 0, 0), ("p", -3, 0, 1, 1), ("p", 2, 1, 1, 1), ("p", 3, 0, 0, 1),
    ("p", -3, 0, 0, 1), ("p", 2, 1, 0, 1), ("p", 2, 0, 1, 0), ("p", -2, 0, 1, 0), ("p", -2, 1, 0, 1),
    ("p", -2, 0, 0, 0), ("p", 2, 0, 0, 0), ("p", -1, 1, 0, 1), ("p", -2, 0, 1, 1), ("p", 2, 0, 1, 1),
    ("p", -1, 1, 1, 1), ("p", 2, 0, 0, 1), ("p", -1, 0, 1, 0), ("p", 0, 1, 1, 0), ("p", 1, 0, 1, 0),
    ("p", -2, 0, 0, 1), ("p", 0, 1, 0, 0), ("p", 1, 0, 0, 0), ("p", -1, 0, 0, 0), ("p", 0, 1, 1, 1),
    ("p", 1, 0, 1, 1), ("p", -1, 0, 1, 1), ("p", 0, 1, 0, 1), ("p", 1, 0, 0, 1), ("p", 0, 0, 1, 0),
    ("p", -1, 0, 0, 1), ("p", 0, 0, 0, 0), ("p", 0, 0, 1, 1), ("p", 0, 0, 0, 1),
)

OFFSETS = tuple((oz, ox) for ox in range(2) for oz in (0, 1, -1, 2, -2, 3, -3, 4))
INDEX = {o: k for k, o in enumerate(OFFSETS)}
N = len(OFFSETS)
REVERSE = {"up": "down", "down": "up", "across": "across"}


def tree(across):
    parent = {}
    for s in range(2):
        sign = 1 if s == 0 else -1

        def real(oz, sign=sign):
            return 4 if oz == 4 else oz * sign

        for oz in range(-3, 5):
            step = 1 if oz > 0 else -1
            hop = ("up" if step * sign > 0 else "down", real(oz - step))
            if oz != 0:
                parent[(real(oz), 0), s] = (hop[0], (hop[1], 0))
            if oz in across:
                parent[(real(oz), 1), s] = ("across", (real(oz), 0))
            else:
                parent[(real(oz), 1), s] = (hop[0], (hop[1], 1))
    return parent


GATHER_TREE = tree(GATHER_ACROSS)
SUM_TREE = tree(SUM_ACROSS)


def children(o, s):
    return [c for (c, r), (_, p) in SUM_TREE.items() if (p, r) == (o, s)]


def pick(k, table):
    got = jnp.int32(table[0])
    for at in range(1, len(table)):
        got = jnp.where(k == at, jnp.int32(table[at]), got)
    return got


def encoded(offsets):
    return [(oz % NZ) * 2 + ox for oz, ox in offsets]


def kernel(
    tok_hbm, tgt_hbm, w_hbm, mom_hbm, nw_hbm, nm_hbm,
    x_own, x_oth, wfull, acc, tgt, mom, cot_own, cot_par, gbuf, sbuf, rbuf,
    dec, gsum, w_t, upd, nm,
    load_sem, out_sem, send_sem, zx_sem, fin_sem, core_sem, tok_sem, cot_sem, rs_sem, ex_sem, up_sem,
):
    g = lax.axis_index("group")
    f = lax.axis_index("fsdp")
    xh, y = g // NY, g % NY
    z, xl, c = f // (NX * NC), (f // NC) % NX, f % NC

    def at(zz, xx, cc):
        return (zz * NX + xx) * NC + cc

    to = {
        "up": {"group": g, "fsdp": at((z + 1) % NZ, xl, c)},
        "down": {"group": g, "fsdp": at((z + NZ - 1) % NZ, xl, c)},
        "across": {"group": g, "fsdp": at(z, 1 - xl, c)},
        "core": {"group": g, "fsdp": at(z, xl, 1 - c)},
        "y_up": {"group": xh * NY + (y + 1) % NY, "fsdp": f},
        "y_down": {"group": xh * NY + (y + NY - 1) % NY, "fsdp": f},
        "beyond": {"group": (1 - xh) * NY + y, "fsdp": at(z, 1 - xl, c)},
    }

    barrier = pltpu.get_barrier_semaphore()
    for name in to:
        pl.semaphore_signal(barrier, inc=1, device_id=to[name], device_id_type=MESH)

    def send(src, dst, s_sem, r_sem, device):
        pltpu.make_async_remote_copy(
            src_ref=src, dst_ref=dst, send_sem=s_sem, recv_sem=r_sem, device_id=device, device_id_type=MESH
        ).start()

    def wait(ref, sem):
        pltpu.make_async_copy(ref, ref, sem).wait()

    def chip_of(enc):
        return (z + NZ - enc // 2) % NZ, (xl + enc) % 2

    def shard_of(o):
        zz, xx = chip_of((o[0] % NZ) * 2 + o[1])
        return at(zz, xx, c)

    w_load = pltpu.make_async_copy(w_hbm, wfull.at[pl.ds(pl.multiple_of(f * ROWS, ROWS), ROWS)], load_sem.at[0])
    w_load.start()

    @pl.loop(0, NZ * NX * NC)
    def _(j):
        pltpu.make_async_copy(
            tok_hbm.at[:, pl.ds(pl.multiple_of(j * ROWS, ROWS), ROWS)], x_own.at[j], load_sem.at[1]
        ).start()

    t_load = pltpu.make_async_copy(tgt_hbm, tgt, load_sem.at[2])
    t_load.start()
    m_load = pltpu.make_async_copy(mom_hbm, mom, load_sem.at[3])
    m_load.start()

    pl.semaphore_wait(barrier, len(to))

    mine = pl.multiple_of(((y + xh) % 2) * HALF, HALF)
    theirs = pl.multiple_of(HALF - mine, HALF)

    def rows(o, start, count):
        return wfull.at[pl.ds(pl.multiple_of(shard_of(o) * ROWS + start, 16), count)]

    def source(o, start, count):
        return w_hbm.at[pl.ds(pl.multiple_of(start, 16), count)] if o == (0, 0) else rows(o, start, count)

    arrived = set()

    def have(o, s, q):
        if o != (0, 0) and (o, s, q) not in arrived:
            arrived.add((o, s, q))
            wait(rows(o, mine + (s * QG + q) * PIECE, PIECE), zx_sem.at[INDEX[o], s, q])

    def gather_op(op):
        kind, o = op[0], (op[1], op[2])
        k = INDEX[o]
        if kind == "s":
            s, q = op[3:]
            direction, before = GATHER_TREE[o, s]
            have(before, s, q)
            start = mine + (s * QG + q) * PIECE
            send(
                source(before, start, PIECE), rows(before, start, PIECE),
                send_sem.at[0], zx_sem.at[k, s, q], to[direction],
            )
        elif kind == "f":
            s = op[3]
            for q in range(QG):
                have(o, s, q)
            start = mine + s * (HALF // 2)
            for name, count in zip(("y_up", "y_down", "beyond"), SPLITS[SPLIT_AT[o[0] % NZ]][s]):
                there = (o[0], 1 - o[1]) if name == "beyond" else o
                if there != (0, 0):
                    send(
                        source(o, start, count), rows(o, start, count),
                        send_sem.at[0], fin_sem.at[INDEX[there]], to[name],
                    )
                start = start + count
        elif kind == "c":
            if o != (0, 0):
                wait(rows(o, theirs, HALF), fin_sem.at[k])
            send(source(o, 0, ROWS), rows(o, 0, ROWS), send_sem.at[0], core_sem.at[k], to["core"])

    first = next(n for n, op in enumerate(GATHER) if op[0] == "f")
    for op in GATHER[:first]:
        gather_op(op)

    @pl.loop(0, N)
    def _(j):
        send(
            tok_hbm.at[:, pl.ds(pl.multiple_of((j * NC + 1 - c) * ROWS, ROWS), ROWS)],
            x_oth.at[j], send_sem.at[1], tok_sem.at[0], to["core"],
        )

    acc[...] = jnp.zeros_like(acc)
    groups, order = [[]], []
    for op in GATHER[first:]:
        if op[0] == "d":
            order.append((op[1], op[2]))
            groups.append([])
        else:
            groups[-1].append(op)

    @pl.loop(0, N)
    def _(t):
        for n in range(N):
            if groups[n]:
                @pl.when(t == n)
                def _(n=n):
                    for op in groups[n]:
                        gather_op(op)

        @pl.when(t == 0)
        def _():
            w_load.wait()
            wait(x_own, load_sem.at[1])

        zz, xx = chip_of(pick(t, encoded(order)))
        k = pick(t, [INDEX[o] for o in order])
        a, b = at(zz, xx, c), at(zz, xx, 1 - c)
        rows_a = pl.ds(pl.multiple_of(a * ROWS, ROWS), ROWS)
        rows_b = pl.ds(pl.multiple_of(b * ROWS, ROWS), ROWS)
        wait(wfull.at[rows_b], core_sem.at[k])
        acc[...] += jnp.dot(x_own[a], wfull[rows_a, :], preferred_element_type=F32) + jnp.dot(
            x_own[b], wfull[rows_b, :], preferred_element_type=F32
        )

    root_width = math.sqrt(D)
    grad_scale = math.sqrt(D / (TOK * NZ * NX * NC))
    t_load.wait()
    for h in range(2):
        toks = slice(h * (TOK // 2), (h + 1) * (TOK // 2))
        cot = (acc[toks, :] / root_width - tgt[toks, :].astype(F32)) * grad_scale
        cot_own[h] = cot.T.astype(BF16)
        send(cot_own.at[h], cot_par.at[h], send_sem.at[2], cot_sem.at[0], to["core"])

    w_t[...] = wfull[pl.ds(pl.multiple_of(f * ROWS, ROWS), ROWS), :].astype(F32).T
    wait(x_oth, tok_sem.at[0])
    wait(cot_par, cot_sem.at[0])

    def total(o, s, q):
        part = pl.ds(q * PART, PART)
        got = gbuf[INDEX[o], s, part, :]
        for child in children(o, s):
            kc = INDEX[child]
            wait(rbuf.at[kc, s, part], rs_sem.at[kc, s, q])
            got = got + rbuf[kc, s, part, :].astype(F32)
        return got

    def owner_part(s, q):
        part = pl.ds(q * PART, PART)
        delta = (inner_rate * (total((0, 0), s, q) / root_width)).reshape(PART // BLOCK, BLOCK, LANES)
        largest = jnp.max(jnp.abs(delta), axis=1, keepdims=True)
        block_scale = jnp.exp2(jnp.ceil(jnp.log2(largest / 6.0 + 1e-30))).astype(BF16).astype(F32)
        code = jnp.clip(delta / block_scale, -6.0, 6.0).astype(BF16)
        dec[s, part, :] = (code.astype(F32) * block_scale).reshape(PART, LANES).astype(BF16)
        for j in range(q * PART // OWN, (q + 1) * PART // OWN):
            @pl.when(g != j)
            def _(j=j):
                send(
                    dec.at[s, pl.ds(j * OWN, OWN)], gsum.at[s, g],
                    send_sem.at[4], ex_sem.at[s], {"group": j, "fsdp": f},
                )

            @pl.when(g == j)
            def _(j=j):
                gsum[s, g] = dec[s, pl.ds(j * OWN, OWN), :]

    def sum_op(op):
        o, s, q = (op[1], op[2]), op[3], op[4]
        if o == (0, 0):
            owner_part(s, q)
            return
        k, part = INDEX[o], pl.ds(q * PART, PART)
        if children(o, s):
            sbuf[k, s, part, :] = total(o, s, q).astype(BF16)
        send(
            sbuf.at[k, s, part], rbuf.at[k, s, part],
            send_sem.at[3], rs_sem.at[k, s, q], to[REVERSE[SUM_TREE[o, s][0]]],
        )

    sum_groups, sum_order = [[]], []
    for op in SUM:
        if op[0] == "u":
            sum_order.append((op[1], op[2]))
            sum_groups.append([])
        else:
            sum_groups[-1].append(op)

    @pl.loop(0, N)
    def _(t):
        zz, xx = chip_of(pick(t, encoded(sum_order)))
        k = pick(t, [INDEX[o] for o in sum_order])
        x_a, x_b = x_own[at(zz, xx, c)], x_oth[zz * NX + xx]
        half = TOK // 2
        grad = jnp.dot(cot_own[0], x_a[:half], preferred_element_type=F32)
        grad += jnp.dot(cot_own[1], x_a[half:], preferred_element_type=F32)
        grad += jnp.dot(cot_par[0], x_b[:half], preferred_element_type=F32)
        grad += jnp.dot(cot_par[1], x_b[half:], preferred_element_type=F32)
        for s in range(2):
            gbuf[k, s] = grad[:, s * LANES : (s + 1) * LANES]
            sbuf[k, s] = grad[:, s * LANES : (s + 1) * LANES].astype(BF16)
        for n in range(N - 1):
            if sum_groups[n + 1]:
                @pl.when(t == n)
                def _(n=n):
                    for op in sum_groups[n + 1]:
                        sum_op(op)

    for op in sum_groups[N]:
        sum_op(op)

    m_load.wait()
    mine_rows = pl.multiple_of(g * OWN, OWN)
    tail = [op[3] for op in SUM if op[0] == "p" and (op[1], op[2]) == (0, 0)]
    turn = (1 - tail[-1], tail[-1])
    for s in turn:
        wait(gsum.at[s, pl.ds(0, NG - 1)], ex_sem.at[s])
        summed = gsum[s, 0].astype(F32)
        for step in range(1, NG):
            summed = summed + gsum[s, step].astype(F32)
        average = summed / NG
        lanes = slice(s * LANES, (s + 1) * LANES)
        new_mom = momentum_decay * mom[:, lanes] + average
        own_w = w_t[pl.ds(mine_rows, OWN), lanes]
        upd[s] = (own_w - outer_rate * (average + momentum_decay * new_mom)).astype(BF16)
        for step in range(1, NG):
            send(
                upd.at[s], nw_hbm.at[pl.ds(mine_rows, OWN), pl.ds(s * LANES, LANES)], send_sem.at[5], up_sem.at[0],
                {"group": (g + step) % NG, "fsdp": f},
            )
        pltpu.make_async_copy(
            upd.at[s], nw_hbm.at[pl.ds(mine_rows, OWN), pl.ds(s * LANES, LANES)], out_sem.at[1]
        ).start()
        nm[:, lanes] = new_mom
    nm_out = pltpu.make_async_copy(nm, nm_hbm, out_sem.at[0])
    nm_out.start()

    wait(wfull.at[pl.ds(0, (N - 1) * ROWS + N * ROWS)], send_sem.at[0])
    wait(x_oth, send_sem.at[1])
    wait(cot_own, send_sem.at[2])
    wait(sbuf.at[pl.ds(0, N - 1)], send_sem.at[3])
    wait(gsum.at[:, pl.ds(0, NG - 1)], send_sem.at[4])
    wait(gsum.at[:, pl.ds(0, NG - 1)], send_sem.at[5])
    nm_out.wait()
    wait(upd, out_sem.at[1])
    wait(gsum.at[:, pl.ds(0, NG - 1)], up_sem.at[0])


def finish(nw_t, nm_t, nw, nm):
    nw[...] = nw_t[...].astype(F32).T.astype(BF16)
    nm[...] = nm_t[...]


def body(tokens, target, weight, momentum):
    hbm = pl.BlockSpec(memory_space=pl.ANY)
    dma = pltpu.SemaphoreType.DMA
    nw_t, nm_t = pl.pallas_call(
        kernel,
        out_shape=(
            jax.ShapeDtypeStruct((KVW, ROWS), BF16),
            jax.ShapeDtypeStruct((OWN, ROWS), F32),
        ),
        in_specs=[hbm] * 4,
        out_specs=(hbm, hbm),
        scratch_shapes=[
            pltpu.VMEM((NZ * NX * NC, TOK, ROWS), BF16),
            pltpu.VMEM((N, TOK, ROWS), BF16),
            pltpu.VMEM((D, KVW), BF16),
            pltpu.VMEM((TOK, KVW), F32),
            pltpu.VMEM((TOK, KVW), BF16),
            pltpu.VMEM((OWN, ROWS), F32),
            pltpu.VMEM((2, KVW, TOK // 2), BF16),
            pltpu.VMEM((2, KVW, TOK // 2), BF16),
            pltpu.VMEM((N, 2, KVW, LANES), F32),
            pltpu.VMEM((N, 2, KVW, LANES), BF16),
            pltpu.VMEM((N, 2, KVW, LANES), BF16),
            pltpu.VMEM((2, KVW, LANES), BF16),
            pltpu.VMEM((2, NG, OWN, LANES), BF16),
            pltpu.VMEM((KVW, ROWS), F32),
            pltpu.VMEM((2, OWN, LANES), BF16),
            pltpu.VMEM((OWN, ROWS), F32),
            dma((4,)), dma((2,)), dma((6,)), dma((N, 2, QG)), dma((N,)), dma((N,)), dma((1,)), dma((1,)),
            dma((N, 2, QR)), dma((2,)), dma((1,)),
        ],
        compiler_params=pltpu.CompilerParams(
            collective_id=0, has_side_effects=True, vmem_limit_bytes=56 * 1024 * 1024
        ),
        cost_estimate=pl.CostEstimate(
            flops=4 * TOK * D * KVW, bytes_accessed=2 * TOK * D + 4 * ROWS * KVW, transcendentals=0
        ),
    )(tokens, target, weight, momentum.T)
    new_weight, new_momentum_t = pl.pallas_call(
        finish,
        out_shape=(
            jax.ShapeDtypeStruct((ROWS, KVW), BF16),
            jax.ShapeDtypeStruct((OWN, ROWS), F32),
        ),
    )(nw_t, nm_t)
    return (new_weight, new_momentum_t.T)


def solution(mesh):
    placed = (
        P(("group", "fsdp"), None),
        P(("group", "fsdp"), None),
        P("fsdp", None),
        P("fsdp", "group"),
    )
    return jax.shard_map(
        body,
        mesh=mesh,
        in_specs=placed,
        out_specs=(P("fsdp", None), P("fsdp", "group")),
        check_vma=False,
    )
```

```python
import math

import jax
import jax.numpy as jnp
from jax import lax
from jax.experimental import pallas as pl
from jax.experimental.pallas import tpu as pltpu
from jax.sharding import PartitionSpec as P

BLOCK = 32
inner_rate = 0.5
momentum_decay = 0.9
outer_rate = 0.7

MESH = pl.DeviceIdType.MESH
F32 = jnp.float32
BF16 = jnp.bfloat16

NZ, NX, NC, NY, NH = 8, 2, 2, 4, 2
NG = NY * NH
D, KVW, TOK = 8192, 512, 512
ROWS = D // (NZ * NX * NC)
HALF = ROWS // 2
OWN = KVW // NG
LANES = 128
QG, QR = 2, 2
PIECE = HALF // 2 // QG
PART = KVW // QR
WIDTH = OWN // QR

GATHER_ACROSS = (-2, -1, 0, 1, 3, 4)
SPLIT = {
    (-3, 0, 0): (0, 64, 0), (-3, 0, 1): (16, 48, 0), (-3, 1, 0): (0, 64, 0), (-3, 1, 1): (64, 0, 0),
    (-2, 0, 0): (64, 0, 0), (-2, 0, 1): (48, 16, 0), (-2, 1, 0): (0, 0, 64), (-2, 1, 1): (64, 0, 0),
    (-1, 0, 0): (16, 48, 0), (-1, 0, 1): (32, 32, 0), (-1, 1, 0): (16, 32, 16), (-1, 1, 1): (16, 16, 32),
    (0, 0, 0): (64, 0, 0), (0, 0, 1): (32, 32, 0), (0, 1, 0): (16, 16, 32), (0, 1, 1): (32, 16, 16),
    (1, 0, 0): (32, 16, 16), (1, 0, 1): (32, 32, 0), (1, 1, 0): (32, 16, 16), (1, 1, 1): (0, 0, 64),
    (2, 0, 0): (16, 48, 0), (2, 0, 1): (16, 48, 0), (2, 1, 0): (0, 0, 64), (2, 1, 1): (0, 0, 64),
    (3, 0, 0): (32, 32, 0), (3, 0, 1): (32, 32, 0), (3, 1, 0): (0, 0, 64), (3, 1, 1): (0, 0, 64),
    (4, 0, 0): (32, 32, 0), (4, 0, 1): (32, 32, 0), (4, 1, 0): (0, 0, 64), (4, 1, 1): (0, 0, 64),
}
GATHER = (
    ("s", -1, 0, 1, 0), ("s", 0, 1, 1, 0), ("s", -1, 0, 1, 1), ("s", 0, 1, 1, 1), ("s", 1, 0, 0, 0),
    ("s", 1, 0, 0, 1), ("s", -1, 0, 0, 0), ("f", 0, 0, 0), ("f", 0, 0, 1), ("s", 0, 1, 0, 0), ("s", 1, 0, 1, 0),
    ("c", 0, 0), ("s", -1, 0, 0, 1), ("s", 0, 1, 0, 1), ("s", 1, 0, 1, 1), ("s", -2, 0, 1, 0), ("s", -1, 1, 1, 0),
    ("s", 2, 0, 0, 0), ("s", 1, 1, 0, 0), ("f", 0, 1, 1), ("s", -2, 0, 1, 1), ("f", -1, 0, 1), ("s", 2, 0, 0, 1),
    ("f", 1, 0, 0), ("s", 1, 1, 0, 1), ("s", -1, 1, 1, 1), ("s", -2, 0, 0, 0), ("s", -1, 1, 0, 0),
    ("s", 2, 0, 1, 0), ("f", 0, 1, 0), ("s", -2, 0, 0, 1), ("f", -1, 0, 0), ("s", -1, 1, 0, 1), ("s", 2, 0, 1, 1),
    ("f", 1, 0, 1), ("s", 1, 1, 1, 0), ("s", -2, 1, 1, 0), ("s", -3, 0, 1, 0), ("s", 3, 0, 0, 0), ("s", 1, 1, 1, 1),
    ("s", 2, 1, 0, 0), ("f", -2, 0, 1), ("s", -3, 0, 1, 1), ("f", 2, 0, 0), ("s", 3, 0, 0, 1), ("f", 1, 1, 0),
    ("s", -2, 1, 0, 0), ("s", 2, 1, 0, 1), ("s", -3, 0, 0, 0), ("s", 3, 0, 1, 0), ("s", 2, 1, 1, 0),
    ("f", -1, 1, 1), ("s", -2, 1, 1, 1), ("f", -2, 0, 0), ("s", -3, 0, 0, 1), ("d", 0, 0), ("s", -2, 1, 0, 1),
    ("f", 2, 0, 1), ("s", 3, 0, 1, 1), ("c", 0, 1), ("c", -1, 0), ("s", 2, 1, 1, 1), ("f", -1, 1, 0),
    ("s", 4, 0, 0, 0), ("s", 4, 0, 1, 0), ("s", -3, 1, 1, 0), ("f", -3, 0, 1), ("s", 4, 0, 1, 1), ("d", 0, 1),
    ("s", 4, 0, 0, 1), ("s", -3, 1, 1, 1), ("f", 3, 0, 0), ("f", 1, 1, 1), ("s", 3, 1, 0, 0), ("s", -3, 1, 0, 0),
    ("f", 2, 1, 0), ("d", -1, 0), ("f", -2, 1, 1), ("s", 3, 1, 0, 1), ("s", 3, 1, 1, 0), ("c", 1, 0), ("c", 1, 1),
    ("f", -3, 0, 0), ("s", -3, 1, 0, 1), ("f", 3, 0, 1), ("f", -2, 1, 0), ("s", 4, 1, 1, 0), ("s", 3, 1, 1, 1),
    ("s", 4, 1, 0, 0), ("f", 2, 1, 1), ("d", 1, 0), ("s", 4, 1, 1, 1), ("f", 4, 0, 0), ("f", 4, 0, 1), ("c", 2, 0),
    ("c", -1, 1), ("c", 2, 1), ("c", -2, 0), ("s", 4, 1, 0, 1), ("d", 1, 1), ("f", -3, 1, 1), ("f", -3, 1, 0),
    ("d", 2, 0), ("f", 3, 1, 0), ("d", -1, 1), ("f", 3, 1, 1), ("c", -3, 0), ("c", -2, 1), ("d", 2, 1), ("c", 3, 0),
    ("c", 3, 1), ("d", -2, 0), ("f", 4, 1, 1), ("d", -3, 0), ("c", 4, 0), ("d", -2, 1), ("f", 4, 1, 0), ("d", 3, 0),
    ("c", 4, 1), ("d", 3, 1), ("c", -3, 1), ("d", 4, 0), ("d", 4, 1), ("d", -3, 1),
)

SUM_ACROSS = (-2, -1, 0, 1, 2)
SUM = (
    ("u", 1, 1), ("p", 1, 1, 0, 0), ("p", 1, 1, 0, 1), ("u", 4, 1), ("p", 4, 1, 0, 0), ("p", 4, 1, 1, 0),
    ("p", 4, 1, 0, 1), ("p", 4, 1, 1, 1), ("u", 2, 0), ("u", -1, 0), ("p", 1, 1, 1, 0), ("u", 3, 1),
    ("p", 3, 1, 1, 0), ("u", -3, 1), ("p", -3, 1, 0, 0), ("u", -2, 1), ("p", 1, 1, 1, 1), ("u", 4, 0),
    ("p", 4, 0, 0, 0), ("p", 4, 0, 1, 0), ("u", -1, 1), ("u", 1, 0), ("p", -1, 1, 0, 0), ("u", -3, 0),
    ("p", 3, 1, 0, 0), ("p", -3, 1, 1, 0), ("u", 0, 0), ("p", -1, 1, 1, 0), ("u", 2, 1), ("u", 0, 1),
    ("p", 3, 1, 0, 1), ("p", -3, 1, 1, 1), ("u", 3, 0), ("p", 2, 1, 1, 0), ("u", -2, 0), ("p", 4, 0, 0, 1),
    ("p", 4, 0, 1, 1), ("p", -2, 1, 0, 0), ("p", 3, 1, 1, 1), ("p", -3, 0, 1, 0), ("p", -2, 1, 1, 0),
    ("p", 3, 0, 1, 0), ("p", -3, 0, 0, 0), ("p", -2, 1, 1, 1), ("p", 3, 0, 1, 1), ("p", -3, 1, 0, 1),
    ("p", 2, 1, 0, 0), ("p", 3, 0, 0, 0), ("p", -3, 0, 1, 1), ("p", 2, 1, 1, 1), ("p", 3, 0, 0, 1),
    ("p", -3, 0, 0, 1), ("p", 2, 1, 0, 1), ("p", 2, 0, 1, 0), ("p", -2, 0, 1, 0), ("p", -2, 1, 0, 1),
    ("p", -2, 0, 0, 0), ("p", 2, 0, 0, 0), ("p", -1, 1, 0, 1), ("p", -2, 0, 1, 1), ("p", 2, 0, 1, 1),
    ("p", -1, 1, 1, 1), ("p", 2, 0, 0, 1), ("p", -1, 0, 1, 0), ("p", 0, 1, 1, 0), ("p", 1, 0, 1, 0),
    ("p", -2, 0, 0, 1), ("p", 0, 1, 0, 0), ("p", 1, 0, 0, 0), ("p", -1, 0, 0, 0), ("p", 0, 1, 1, 1),
    ("p", 1, 0, 1, 1), ("p", -1, 0, 1, 1), ("p", 0, 1, 0, 1), ("p", 1, 0, 0, 1), ("p", 0, 0, 1, 0),
    ("p", -1, 0, 0, 1), ("p", 0, 0, 0, 0), ("p", 0, 0, 1, 1), ("p", 0, 0, 0, 1),
)

OFFSETS = tuple((oz, ox) for ox in range(2) for oz in (0, 1, -1, 2, -2, 3, -3, 4))
INDEX = {o: k for k, o in enumerate(OFFSETS)}
N = len(OFFSETS)
REVERSE = {"up": "down", "down": "up", "across": "across"}


def tree(across):
    parent = {}
    for s in range(2):
        sign = 1 if s == 0 else -1

        def real(oz, sign=sign):
            return 4 if oz == 4 else oz * sign

        for oz in range(-3, 5):
            step = 1 if oz > 0 else -1
            hop = ("up" if step * sign > 0 else "down", real(oz - step))
            if oz != 0:
                parent[(real(oz), 0), s] = (hop[0], (hop[1], 0))
            if oz in across:
                parent[(real(oz), 1), s] = ("across", (real(oz), 0))
            else:
                parent[(real(oz), 1), s] = (hop[0], (hop[1], 1))
    return parent


GATHER_TREE = tree(GATHER_ACROSS)
SUM_TREE = tree(SUM_ACROSS)


def children(o, s):
    return [c for (c, r), (_, p) in SUM_TREE.items() if (p, r) == (o, s)]


def pick(k, table):
    got = jnp.int32(table[0])
    for at in range(1, len(table)):
        got = jnp.where(k == at, jnp.int32(table[at]), got)
    return got


def encoded(offsets):
    return [(oz % NZ) * 2 + ox for oz, ox in offsets]


def kernel(
    tok_hbm, tgt_hbm, w_hbm, mom_hbm, nw_hbm, nm_hbm,
    x_own, x_oth, wfull, acc, tgt, mom, cot_own, cot_par, gbuf, sbuf, rbuf,
    dec, gsum, w_t, upd, nm,
    load_sem, out_sem, send_sem, zx_sem, fin_sem, core_sem, tok_sem, cot_sem, rs_sem, ex_sem, up_sem,
):
    g = lax.axis_index("group")
    f = lax.axis_index("fsdp")
    xh, y = g // NY, g % NY
    z, xl, c = f // (NX * NC), (f // NC) % NX, f % NC

    def at(zz, xx, cc):
        return (zz * NX + xx) * NC + cc

    to = {
        "up": {"group": g, "fsdp": at((z + 1) % NZ, xl, c)},
        "down": {"group": g, "fsdp": at((z + NZ - 1) % NZ, xl, c)},
        "across": {"group": g, "fsdp": at(z, 1 - xl, c)},
        "core": {"group": g, "fsdp": at(z, xl, 1 - c)},
        "y_up": {"group": xh * NY + (y + 1) % NY, "fsdp": f},
        "y_down": {"group": xh * NY + (y + NY - 1) % NY, "fsdp": f},
        "beyond": {"group": (1 - xh) * NY + y, "fsdp": at(z, 1 - xl, c)},
    }

    barrier = pltpu.get_barrier_semaphore()
    for name in to:
        pl.semaphore_signal(barrier, inc=1, device_id=to[name], device_id_type=MESH)

    def send(src, dst, s_sem, r_sem, device):
        pltpu.make_async_remote_copy(
            src_ref=src, dst_ref=dst, send_sem=s_sem, recv_sem=r_sem, device_id=device, device_id_type=MESH
        ).start()

    def wait(ref, sem):
        pltpu.make_async_copy(ref, ref, sem).wait()

    def chip_of(enc):
        return (z + NZ - enc // 2) % NZ, (xl + enc) % 2

    def shard_of(o):
        zz, xx = chip_of((o[0] % NZ) * 2 + o[1])
        return at(zz, xx, c)

    w_load = pltpu.make_async_copy(w_hbm, wfull.at[pl.ds(pl.multiple_of(f * ROWS, ROWS), ROWS)], load_sem.at[0])
    w_load.start()

    @pl.loop(0, NZ * NX * NC)
    def _(j):
        pltpu.make_async_copy(
            tok_hbm.at[:, pl.ds(pl.multiple_of(j * ROWS, ROWS), ROWS)], x_own.at[j], load_sem.at[1]
        ).start()

    t_load = pltpu.make_async_copy(tgt_hbm, tgt, load_sem.at[2])
    t_load.start()
    m_load = pltpu.make_async_copy(mom_hbm, mom, load_sem.at[3])
    m_load.start()

    pl.semaphore_wait(barrier, len(to))

    mine = pl.multiple_of(((y + xh) % 2) * HALF, HALF)
    theirs = pl.multiple_of(HALF - mine, HALF)

    def rows(o, start, count):
        return wfull.at[pl.ds(pl.multiple_of(shard_of(o) * ROWS + start, 16), count)]

    def source(o, start, count):
        return w_hbm.at[pl.ds(pl.multiple_of(start, 16), count)] if o == (0, 0) else rows(o, start, count)

    arrived = set()

    def have(o, s, q):
        if o != (0, 0) and (o, s, q) not in arrived:
            arrived.add((o, s, q))
            wait(rows(o, mine + (s * QG + q) * PIECE, PIECE), zx_sem.at[INDEX[o], s, q])

    def gather_op(op):
        kind, o = op[0], (op[1], op[2])
        k = INDEX[o]
        if kind == "s":
            s, q = op[3:]
            direction, before = GATHER_TREE[o, s]
            have(before, s, q)
            start = mine + (s * QG + q) * PIECE
            send(
                source(before, start, PIECE), rows(before, start, PIECE),
                send_sem.at[0], zx_sem.at[k, s, q], to[direction],
            )
        elif kind == "f":
            s = op[3]
            for q in range(QG):
                have(o, s, q)
            base = mine + s * (HALF // 2)
            there = (o[0], 1 - o[1])
            near, far = SPLIT[*o, s], SPLIT[*there, s]
            for name, place, start, count in (
                ("y_up", o, 0, near[0]),
                ("y_down", o, near[0], near[1]),
                ("beyond", there, far[0] + far[1], far[2]),
            ):
                if count and place != (0, 0):
                    send(
                        source(o, base + start, count), rows(o, base + start, count),
                        send_sem.at[0], fin_sem.at[INDEX[place]], to[name],
                    )
        elif kind == "c":
            if o != (0, 0):
                wait(rows(o, theirs, HALF), fin_sem.at[k])
            send(source(o, 0, ROWS), rows(o, 0, ROWS), send_sem.at[0], core_sem.at[k], to["core"])

    first = next(n for n, op in enumerate(GATHER) if op[0] == "f")
    for op in GATHER[:first]:
        gather_op(op)

    @pl.loop(0, N)
    def _(j):
        send(
            tok_hbm.at[:, pl.ds(pl.multiple_of((j * NC + 1 - c) * ROWS, ROWS), ROWS)],
            x_oth.at[j], send_sem.at[1], tok_sem.at[0], to["core"],
        )

    acc[...] = jnp.zeros_like(acc)
    groups, order = [[]], []
    for op in GATHER[first:]:
        if op[0] == "d":
            order.append((op[1], op[2]))
            groups.append([])
        else:
            groups[-1].append(op)

    @pl.loop(0, N)
    def _(t):
        for n in range(N):
            if groups[n]:
                @pl.when(t == n)
                def _(n=n):
                    for op in groups[n]:
                        gather_op(op)

        @pl.when(t == 0)
        def _():
            w_load.wait()
            wait(x_own, load_sem.at[1])

        zz, xx = chip_of(pick(t, encoded(order)))
        k = pick(t, [INDEX[o] for o in order])
        a, b = at(zz, xx, c), at(zz, xx, 1 - c)
        rows_a = pl.ds(pl.multiple_of(a * ROWS, ROWS), ROWS)
        rows_b = pl.ds(pl.multiple_of(b * ROWS, ROWS), ROWS)
        wait(wfull.at[rows_b], core_sem.at[k])
        acc[...] += jnp.dot(x_own[a], wfull[rows_a, :], preferred_element_type=F32) + jnp.dot(
            x_own[b], wfull[rows_b, :], preferred_element_type=F32
        )

    root_width = math.sqrt(D)
    grad_scale = math.sqrt(D / (TOK * NZ * NX * NC))
    t_load.wait()
    for h in range(2):
        toks = slice(h * (TOK // 2), (h + 1) * (TOK // 2))
        cot = (acc[toks, :] * (1.0 / root_width) - tgt[toks, :].astype(F32)) * grad_scale
        cot_t = cot.T.astype(BF16)
        for j in range(NG):
            for q in range(QR):
                cot_own[h, q * PART + j * WIDTH : q * PART + (j + 1) * WIDTH, :] = cot_t[
                    j * OWN + q * WIDTH : j * OWN + (q + 1) * WIDTH
                ]
        send(cot_own.at[h], cot_par.at[h], send_sem.at[2], cot_sem.at[0], to["core"])

    w_t[...] = wfull[pl.ds(pl.multiple_of(f * ROWS, ROWS), ROWS), :].astype(F32).T
    wait(x_oth, tok_sem.at[0])
    wait(cot_par, cot_sem.at[0])

    def total(o, s, q):
        part = pl.ds(q * PART, PART)
        got = gbuf[INDEX[o], s, part, :]
        for child in children(o, s):
            kc = INDEX[child]
            wait(rbuf.at[kc, s, part], rs_sem.at[kc, s, q])
            got = got + rbuf[kc, s, part, :].astype(F32)
        return got

    def owner_part(s, q):
        part = pl.ds(q * PART, PART)
        delta = (total((0, 0), s, q) * (inner_rate / root_width)).reshape(PART // BLOCK, BLOCK, LANES)
        largest = jnp.max(jnp.abs(delta), axis=1, keepdims=True)
        block_scale = jnp.exp2(jnp.ceil(jnp.log2(largest / 6.0 + 1e-30))).astype(BF16).astype(F32)
        code = jnp.clip(delta * (1.0 / block_scale), -6.0, 6.0).astype(BF16)
        dec[s, part, :] = (code.astype(F32) * block_scale).reshape(PART, LANES).astype(BF16)
        for step in range(1, NG):
            other = (g + step) % NG
            send(
                dec.at[s, pl.ds(pl.multiple_of(q * PART + other * WIDTH, WIDTH), WIDTH)],
                gsum.at[s, g, pl.ds(q * WIDTH, WIDTH)], send_sem.at[4], ex_sem.at[s], {"group": other, "fsdp": f},
            )
        gsum[s, g, pl.ds(q * WIDTH, WIDTH), :] = dec[s, pl.ds(pl.multiple_of(q * PART + g * WIDTH, WIDTH), WIDTH), :]

    def sum_op(op):
        o, s, q = (op[1], op[2]), op[3], op[4]
        if o == (0, 0):
            owner_part(s, q)
            return
        k, part = INDEX[o], pl.ds(q * PART, PART)
        if children(o, s):
            sbuf[k, s, part, :] = total(o, s, q).astype(BF16)
        send(
            sbuf.at[k, s, part], rbuf.at[k, s, part],
            send_sem.at[3], rs_sem.at[k, s, q], to[REVERSE[SUM_TREE[o, s][0]]],
        )

    sum_groups, sum_order = [[]], []
    for op in SUM:
        if op[0] == "u":
            sum_order.append((op[1], op[2]))
            sum_groups.append([])
        else:
            sum_groups[-1].append(op)

    @pl.loop(0, N)
    def _(t):
        zz, xx = chip_of(pick(t, encoded(sum_order)))
        k = pick(t, [INDEX[o] for o in sum_order])
        x_a, x_b = x_own[at(zz, xx, c)], x_oth[zz * NX + xx]
        half = TOK // 2
        grad = jnp.dot(cot_own[0], x_a[:half], preferred_element_type=F32)
        grad += jnp.dot(cot_own[1], x_a[half:], preferred_element_type=F32)
        grad += jnp.dot(cot_par[0], x_b[:half], preferred_element_type=F32)
        grad += jnp.dot(cot_par[1], x_b[half:], preferred_element_type=F32)
        for s in range(2):
            gbuf[k, s] = grad[:, s * LANES : (s + 1) * LANES]
            sbuf[k, s] = grad[:, s * LANES : (s + 1) * LANES].astype(BF16)
        for n in range(N - 1):
            if sum_groups[n + 1]:
                @pl.when(t == n)
                def _(n=n):
                    for op in sum_groups[n + 1]:
                        sum_op(op)

    for op in sum_groups[N]:
        sum_op(op)

    m_load.wait()
    mine_rows = pl.multiple_of(g * OWN, OWN)
    tail = [op[3] for op in SUM if op[0] == "p" and (op[1], op[2]) == (0, 0)]
    turn = (1 - tail[-1], tail[-1])
    for s in turn:
        wait(gsum.at[s, pl.ds(0, NG - 1)], ex_sem.at[s])
        summed = gsum[s, 0].astype(F32)
        for step in range(1, NG):
            summed = summed + gsum[s, step].astype(F32)
        average = summed * (1.0 / NG)
        lanes = slice(s * LANES, (s + 1) * LANES)
        new_mom = momentum_decay * mom[:, lanes] + average
        own_w = w_t[pl.ds(mine_rows, OWN), lanes]
        upd[s] = (own_w - outer_rate * (average + momentum_decay * new_mom)).astype(BF16)
        for step in range(1, NG):
            send(
                upd.at[s], nw_hbm.at[pl.ds(mine_rows, OWN), pl.ds(s * LANES, LANES)], send_sem.at[5], up_sem.at[0],
                {"group": (g + step) % NG, "fsdp": f},
            )
        pltpu.make_async_copy(
            upd.at[s], nw_hbm.at[pl.ds(mine_rows, OWN), pl.ds(s * LANES, LANES)], out_sem.at[1]
        ).start()
        nm[:, lanes] = new_mom
    nm_out = pltpu.make_async_copy(nm, nm_hbm, out_sem.at[0])
    nm_out.start()

    wait(wfull.at[pl.ds(0, (N - 1) * ROWS + N * ROWS)], send_sem.at[0])
    wait(x_oth, send_sem.at[1])
    wait(cot_own, send_sem.at[2])
    wait(sbuf.at[pl.ds(0, N - 1)], send_sem.at[3])
    wait(gsum.at[:, pl.ds(0, NG - 1)], send_sem.at[4])
    wait(gsum.at[:, pl.ds(0, NG - 1)], send_sem.at[5])
    nm_out.wait()
    wait(upd, out_sem.at[1])
    wait(gsum.at[:, pl.ds(0, NG - 1)], up_sem.at[0])


def finish(nw_t, nm_t, nw, nm):
    nw[...] = nw_t[...].astype(F32).T.astype(BF16)
    nm[...] = nm_t[...]


def body(tokens, target, weight, momentum):
    hbm = pl.BlockSpec(memory_space=pl.ANY)
    dma = pltpu.SemaphoreType.DMA
    nw_t, nm_t = pl.pallas_call(
        kernel,
        out_shape=(
            jax.ShapeDtypeStruct((KVW, ROWS), BF16),
            jax.ShapeDtypeStruct((OWN, ROWS), F32),
        ),
        in_specs=[hbm] * 4,
        out_specs=(hbm, hbm),
        scratch_shapes=[
            pltpu.VMEM((NZ * NX * NC, TOK, ROWS), BF16),
            pltpu.VMEM((N, TOK, ROWS), BF16),
            pltpu.VMEM((D, KVW), BF16),
            pltpu.VMEM((TOK, KVW), F32),
            pltpu.VMEM((TOK, KVW), BF16),
            pltpu.VMEM((OWN, ROWS), F32),
            pltpu.VMEM((2, KVW, TOK // 2), BF16),
            pltpu.VMEM((2, KVW, TOK // 2), BF16),
            pltpu.VMEM((N, 2, KVW, LANES), F32),
            pltpu.VMEM((N, 2, KVW, LANES), BF16),
            pltpu.VMEM((N, 2, KVW, LANES), BF16),
            pltpu.VMEM((2, KVW, LANES), BF16),
            pltpu.VMEM((2, NG, OWN, LANES), BF16),
            pltpu.VMEM((KVW, ROWS), F32),
            pltpu.VMEM((2, OWN, LANES), BF16),
            pltpu.VMEM((OWN, ROWS), F32),
            dma((4,)), dma((2,)), dma((6,)), dma((N, 2, QG)), dma((N,)), dma((N,)), dma((1,)), dma((1,)),
            dma((N, 2, QR)), dma((2,)), dma((1,)),
        ],
        compiler_params=pltpu.CompilerParams(
            collective_id=0, has_side_effects=True, vmem_limit_bytes=56 * 1024 * 1024
        ),
        cost_estimate=pl.CostEstimate(
            flops=4 * TOK * D * KVW, bytes_accessed=2 * TOK * D + 4 * ROWS * KVW, transcendentals=0
        ),
    )(tokens, target, weight, momentum.T)
    new_weight, new_momentum_t = pl.pallas_call(
        finish,
        out_shape=(
            jax.ShapeDtypeStruct((ROWS, KVW), BF16),
            jax.ShapeDtypeStruct((OWN, ROWS), F32),
        ),
    )(nw_t, nm_t)
    return (new_weight, new_momentum_t.T)


def solution(mesh):
    placed = (
        P(("group", "fsdp"), None),
        P(("group", "fsdp"), None),
        P("fsdp", None),
        P("fsdp", "group"),
    )
    return jax.shard_map(
        body,
        mesh=mesh,
        in_specs=placed,
        out_specs=(P("fsdp", None), P("fsdp", "group")),
        check_vma=False,
    )
```

```python
import functools
import math

import jax
import jax.numpy as jnp
from jax import lax
from jax.experimental import pallas as pl
from jax.experimental.pallas import tpu as pltpu
from jax.sharding import PartitionSpec as P

BLOCK = 32
inner_rate = 0.5
momentum_decay = 0.9
outer_rate = 0.7

MESH = pl.DeviceIdType.MESH
F32 = jnp.float32
BF16 = jnp.bfloat16

NZ, NX, NC, NY, NH = 8, 2, 2, 4, 2
NG = NY * NH
D, KVW, TOK = 8192, 512, 512
ROWS = D // (NZ * NX * NC)
HALF = ROWS // 2
OWN = KVW // NG
LANES = 128
QG, QR = 2, 2
PIECE = HALF // 2 // QG
PART = KVW // QR
WIDTH = OWN // QR

GATHER_TREE = {
    (-3, 0, 0): ("down", (-2, 0)), (-3, 1, 0): ("down", (-2, 1)), (-2, 0, 0): ("down", (-1, 0)), (-2, 1, 0): ("across", (-2, 0)),
    (-1, 0, 0): ("down", (0, 0)), (-1, 1, 0): ("across", (-1, 0)), (0, 1, 0): ("across", (0, 0)), (1, 0, 0): ("up", (0, 0)),
    (1, 1, 0): ("across", (1, 0)), (2, 0, 0): ("up", (1, 0)), (2, 1, 0): ("up", (1, 1)), (3, 0, 0): ("up", (2, 0)),
    (3, 1, 0): ("across", (3, 0)), (4, 0, 0): ("up", (3, 0)), (4, 1, 0): ("across", (4, 0)), (3, 0, 1): ("up", (2, 0)),
    (3, 1, 1): ("up", (2, 1)), (2, 0, 1): ("up", (1, 0)), (2, 1, 1): ("across", (2, 0)), (1, 0, 1): ("up", (0, 0)),
    (1, 1, 1): ("across", (1, 0)), (0, 1, 1): ("across", (0, 0)), (-1, 0, 1): ("down", (0, 0)), (-1, 1, 1): ("across", (-1, 0)),
    (-2, 0, 1): ("down", (-1, 0)), (-2, 1, 1): ("down", (-1, 1)), (-3, 0, 1): ("down", (-2, 0)), (-3, 1, 1): ("across", (-3, 0)),
    (4, 0, 1): ("down", (-3, 0)), (4, 1, 1): ("across", (4, 0)),
}
SPLIT = {
    (-3, 0, 0): (0, 64, 0), (-3, 0, 1): (16, 48, 0), (-3, 1, 0): (0, 64, 0), (-3, 1, 1): (64, 0, 0),
    (-2, 0, 0): (64, 0, 0), (-2, 0, 1): (48, 16, 0), (-2, 1, 0): (0, 0, 64), (-2, 1, 1): (64, 0, 0),
    (-1, 0, 0): (16, 48, 0), (-1, 0, 1): (32, 32, 0), (-1, 1, 0): (16, 32, 16), (-1, 1, 1): (16, 16, 32),
    (0, 0, 0): (64, 0, 0), (0, 0, 1): (32, 32, 0), (0, 1, 0): (16, 16, 32), (0, 1, 1): (32, 16, 16),
    (1, 0, 0): (32, 16, 16), (1, 0, 1): (32, 32, 0), (1, 1, 0): (32, 16, 16), (1, 1, 1): (0, 0, 64),
    (2, 0, 0): (16, 48, 0), (2, 0, 1): (16, 48, 0), (2, 1, 0): (0, 0, 64), (2, 1, 1): (0, 0, 64),
    (3, 0, 0): (32, 32, 0), (3, 0, 1): (32, 32, 0), (3, 1, 0): (0, 0, 64), (3, 1, 1): (0, 0, 64),
    (4, 0, 0): (32, 32, 0), (4, 0, 1): (32, 32, 0), (4, 1, 0): (0, 0, 64), (4, 1, 1): (0, 0, 64),
}
GATHER = (
    ("s", -1, 0, 1, 0), ("s", 0, 1, 1, 0), ("s", -1, 0, 1, 1), ("s", 0, 1, 1, 1), ("s", 1, 0, 0, 0),
    ("s", 1, 0, 0, 1), ("s", -1, 0, 0, 0), ("f", 0, 0, 0), ("f", 0, 0, 1), ("s", 0, 1, 0, 0), ("s", 1, 0, 1, 0),
    ("c", 0, 0), ("s", -1, 0, 0, 1), ("s", 0, 1, 0, 1), ("s", 1, 0, 1, 1), ("s", -2, 0, 1, 0), ("s", -1, 1, 1, 0),
    ("s", 2, 0, 0, 0), ("s", 1, 1, 0, 0), ("f", 0, 1, 1), ("s", -2, 0, 1, 1), ("f", -1, 0, 1), ("s", 2, 0, 0, 1),
    ("f", 1, 0, 0), ("s", 1, 1, 0, 1), ("s", -1, 1, 1, 1), ("s", -2, 0, 0, 0), ("s", -1, 1, 0, 0),
    ("s", 2, 0, 1, 0), ("f", 0, 1, 0), ("s", -2, 0, 0, 1), ("f", -1, 0, 0), ("s", -1, 1, 0, 1), ("s", 2, 0, 1, 1),
    ("f", 1, 0, 1), ("s", 1, 1, 1, 0), ("s", -2, 1, 1, 0), ("s", -3, 0, 1, 0), ("s", 3, 0, 0, 0), ("s", 1, 1, 1, 1),
    ("s", 2, 1, 0, 0), ("f", -2, 0, 1), ("s", -3, 0, 1, 1), ("f", 2, 0, 0), ("s", 3, 0, 0, 1), ("f", 1, 1, 0),
    ("s", -2, 1, 0, 0), ("s", 2, 1, 0, 1), ("s", -3, 0, 0, 0), ("s", 3, 0, 1, 0), ("s", 2, 1, 1, 0),
    ("f", -1, 1, 1), ("s", -2, 1, 1, 1), ("f", -2, 0, 0), ("s", -3, 0, 0, 1), ("d", 0, 0), ("s", -2, 1, 0, 1),
    ("f", 2, 0, 1), ("s", 3, 0, 1, 1), ("c", 0, 1), ("c", -1, 0), ("s", 2, 1, 1, 1), ("f", -1, 1, 0),
    ("s", 4, 0, 0, 0), ("s", 4, 0, 1, 0), ("s", -3, 1, 1, 0), ("f", -3, 0, 1), ("s", 4, 0, 1, 1), ("d", 0, 1),
    ("s", 4, 0, 0, 1), ("s", -3, 1, 1, 1), ("f", 3, 0, 0), ("f", 1, 1, 1), ("s", 3, 1, 0, 0), ("s", -3, 1, 0, 0),
    ("f", 2, 1, 0), ("d", -1, 0), ("f", -2, 1, 1), ("s", 3, 1, 0, 1), ("s", 3, 1, 1, 0), ("c", 1, 0), ("c", 1, 1),
    ("f", -3, 0, 0), ("s", -3, 1, 0, 1), ("f", 3, 0, 1), ("f", -2, 1, 0), ("s", 4, 1, 1, 0), ("s", 3, 1, 1, 1),
    ("s", 4, 1, 0, 0), ("f", 2, 1, 1), ("d", 1, 0), ("s", 4, 1, 1, 1), ("f", 4, 0, 0), ("f", 4, 0, 1), ("c", 2, 0),
    ("c", -1, 1), ("c", 2, 1), ("c", -2, 0), ("s", 4, 1, 0, 1), ("d", 1, 1), ("f", -3, 1, 1), ("f", -3, 1, 0),
    ("d", 2, 0), ("f", 3, 1, 0), ("d", -1, 1), ("f", 3, 1, 1), ("c", -3, 0), ("c", -2, 1), ("d", 2, 1), ("c", 3, 0),
    ("c", 3, 1), ("d", -2, 0), ("f", 4, 1, 1), ("d", -3, 0), ("c", 4, 0), ("d", -2, 1), ("f", 4, 1, 0), ("d", 3, 0),
    ("c", 4, 1), ("d", 3, 1), ("c", -3, 1), ("d", 4, 0), ("d", 4, 1), ("d", -3, 1),
)

SUM_ACROSS = (-2, -1, 0, 1, 2)
SUM = (
    ("u", 4, 1), ("p", 4, 1, 1, 0), ("p", 4, 1, 1, 1), ("p", 4, 1, 0, 0), ("p", 4, 1, 0, 1), ("u", 1, 1),
    ("p", 1, 1, 1, 0), ("p", 1, 1, 1, 1), ("u", -2, 1), ("u", -3, 1), ("p", -3, 1, 0, 0), ("u", 3, 0),
    ("p", 1, 1, 0, 0), ("p", 3, 0, 1, 0), ("u", -2, 0), ("u", 3, 1), ("p", 3, 1, 1, 0), ("p", -3, 1, 0, 1),
    ("u", 0, 0), ("p", 1, 1, 0, 1), ("u", -1, 1), ("u", -1, 0), ("p", 3, 1, 0, 0), ("p", -3, 1, 1, 0), ("u", 1, 0),
    ("p", -1, 1, 0, 0), ("u", 2, 0), ("p", -3, 1, 1, 1), ("p", 3, 1, 0, 1), ("u", 4, 0), ("p", -1, 1, 0, 1),
    ("u", 0, 1), ("u", -3, 0), ("p", 4, 0, 1, 0), ("p", 3, 1, 1, 1), ("u", 2, 1), ("p", -2, 1, 0, 0),
    ("p", 4, 0, 1, 1), ("p", 4, 0, 0, 0), ("p", 2, 1, 1, 0), ("p", -3, 0, 0, 0), ("p", 4, 0, 0, 1),
    ("p", -2, 1, 1, 0), ("p", -3, 0, 0, 1), ("p", 3, 0, 1, 1), ("p", 2, 1, 0, 0), ("p", -3, 0, 1, 0),
    ("p", 2, 1, 1, 1), ("p", 3, 0, 0, 0), ("p", -3, 0, 1, 1), ("p", 2, 0, 1, 0), ("p", -2, 1, 1, 1),
    ("p", -2, 0, 0, 0), ("p", 3, 0, 0, 1), ("p", 2, 1, 0, 1), ("p", -2, 1, 0, 1), ("p", -2, 0, 1, 0),
    ("p", 2, 0, 0, 0), ("p", 2, 0, 1, 1), ("p", -1, 1, 1, 0), ("p", -2, 0, 1, 1), ("p", 1, 0, 1, 0),
    ("p", -1, 1, 1, 1), ("p", -1, 0, 0, 0), ("p", 2, 0, 0, 1), ("p", 0, 1, 1, 0), ("p", -2, 0, 0, 1),
    ("p", 1, 0, 0, 0), ("p", 0, 1, 0, 0), ("p", -1, 0, 1, 0), ("p", 1, 0, 1, 1), ("p", 0, 1, 1, 1),
    ("p", -1, 0, 1, 1), ("p", 0, 1, 0, 1), ("p", 1, 0, 0, 1), ("p", -1, 0, 0, 1), ("p", 0, 0, 1, 0),
    ("p", 0, 0, 0, 0), ("p", 0, 0, 1, 1), ("p", 0, 0, 0, 1),
)

OFFSETS = tuple((oz, ox) for ox in range(2) for oz in (0, 1, -1, 2, -2, 3, -3, 4))
INDEX = {o: k for k, o in enumerate(OFFSETS)}
N = len(OFFSETS)
REVERSE = {"up": "down", "down": "up", "across": "across"}


def tree(across):
    parent = {}
    for s in range(2):
        sign = 1 if s == 0 else -1

        def real(oz, sign=sign):
            return 4 if oz == 4 else oz * sign

        for oz in range(-3, 5):
            step = 1 if oz > 0 else -1
            hop = ("up" if step * sign > 0 else "down", real(oz - step))
            if oz != 0:
                parent[(real(oz), 0), s] = (hop[0], (hop[1], 0))
            if oz in across:
                parent[(real(oz), 1), s] = ("across", (real(oz), 0))
            else:
                parent[(real(oz), 1), s] = (hop[0], (hop[1], 1))
    return parent


SUM_TREE = tree(SUM_ACROSS)


def children(o, s):
    return [c for (c, r), (_, p) in SUM_TREE.items() if (p, r) == (o, s)]


def pick(k, table):
    if len(table) == 1:
        return jnp.int32(table[0])
    half = 1 << (len(table) - 1).bit_length() - 1
    return jnp.where(k < half, pick(k, table[:half]), pick(k - half, table[half:]))


def dispatch(t, acts, width=4):
    for low in range(0, len(acts), width):
        block = [(n, acts[n]) for n in range(low, min(low + width, len(acts))) if acts[n]]
        if block:
            @pl.when((t >= low) & (t < low + width))
            def _(block=block):
                for n, act in block:
                    pl.when(t == n)(act)


def all_of(act, ops):
    for op in ops:
        act(op)


def quo(a, b):
    return lax.div(a, jnp.int32(b))


def rem(a, b):
    return lax.rem(a, jnp.int32(b))


def encoded(offsets):
    return [(oz % NZ) * 2 + ox for oz, ox in offsets]


def kernel(
    tok_hbm, tgt_hbm, w_hbm, mom_hbm, nw_hbm, nm_hbm,
    x_own, x_oth, wfull, acc, tgt, mom, cot_own, cot_par, gbuf, sbuf, rbuf,
    dec, gsum, w_t, upd, nm,
    load_sem, out_sem, send_sem, zx_sem, fin_sem, core_sem, tok_sem, cot_sem, rs_sem, ex_sem, up_sem,
):
    g = lax.axis_index("group")
    f = lax.axis_index("fsdp")
    xh, y = quo(g, NY), rem(g, NY)
    z, xl, c = quo(f, NX * NC), rem(quo(f, NC), NX), rem(f, NC)

    def at(zz, xx, cc):
        return (zz * NX + xx) * NC + cc

    to = {
        "up": {"group": g, "fsdp": at(rem(z + 1, NZ), xl, c)},
        "down": {"group": g, "fsdp": at(rem(z + NZ - 1, NZ), xl, c)},
        "across": {"group": g, "fsdp": at(z, 1 - xl, c)},
        "core": {"group": g, "fsdp": at(z, xl, 1 - c)},
        "y_up": {"group": xh * NY + rem(y + 1, NY), "fsdp": f},
        "y_down": {"group": xh * NY + rem(y + NY - 1, NY), "fsdp": f},
        "beyond": {"group": (1 - xh) * NY + y, "fsdp": at(z, 1 - xl, c)},
    }

    barrier = pltpu.get_barrier_semaphore()
    for name in to:
        pl.semaphore_signal(barrier, inc=1, device_id=to[name], device_id_type=MESH)

    def send(src, dst, s_sem, r_sem, device):
        pltpu.make_async_remote_copy(
            src_ref=src, dst_ref=dst, send_sem=s_sem, recv_sem=r_sem, device_id=device, device_id_type=MESH
        ).start()

    def wait(ref, sem):
        pltpu.make_async_copy(ref, ref, sem).wait()

    def chip_of(enc):
        enc = jnp.int32(enc)
        return rem(z + NZ - quo(enc, 2), NZ), rem(xl + enc, 2)

    def shard_of(o):
        zz, xx = chip_of((o[0] % NZ) * 2 + o[1])
        return at(zz, xx, c)

    w_load = pltpu.make_async_copy(w_hbm, wfull.at[pl.ds(pl.multiple_of(f * ROWS, ROWS), ROWS)], load_sem.at[0])
    w_load.start()

    @pl.loop(0, NZ * NX * NC)
    def _(j):
        pltpu.make_async_copy(
            tok_hbm.at[:, pl.ds(pl.multiple_of(j * ROWS, ROWS), ROWS)], x_own.at[j], load_sem.at[1]
        ).start()

    t_load = pltpu.make_async_copy(tgt_hbm, tgt, load_sem.at[2])
    t_load.start()
    m_load = pltpu.make_async_copy(mom_hbm, mom, load_sem.at[3])
    m_load.start()

    pl.semaphore_wait(barrier, len(to))

    row_of = {o: shard_of(o) * ROWS for o in OFFSETS}
    mine = pl.multiple_of(rem(y + xh, 2) * HALF, HALF)
    theirs = pl.multiple_of(HALF - mine, HALF)

    def rows(o, start, count):
        return wfull.at[pl.ds(pl.multiple_of(row_of[o] + start, 16), count)]

    def source(o, start, count):
        return w_hbm.at[pl.ds(pl.multiple_of(start, 16), count)] if o == (0, 0) else rows(o, start, count)

    arrived = set()

    def have(o, s, q):
        if o != (0, 0) and (o, s, q) not in arrived:
            arrived.add((o, s, q))
            wait(rows(o, mine + (s * QG + q) * PIECE, PIECE), zx_sem.at[INDEX[o], s, q])

    def gather_op(op):
        kind, o = op[0], (op[1], op[2])
        k = INDEX[o]
        if kind == "s":
            s, q = op[3:]
            direction, before = GATHER_TREE[*o, s]
            have(before, s, q)
            start = mine + (s * QG + q) * PIECE
            send(
                source(before, start, PIECE), rows(before, start, PIECE),
                send_sem.at[0], zx_sem.at[k, s, q], to[direction],
            )
        elif kind == "f":
            s = op[3]
            for q in range(QG):
                have(o, s, q)
            base = mine + s * (HALF // 2)
            there = (o[0], 1 - o[1])
            near, far = SPLIT[*o, s], SPLIT[*there, s]
            for name, place, start, count in (
                ("y_up", o, 0, near[0]),
                ("y_down", o, near[0], near[1]),
                ("beyond", there, far[0] + far[1], far[2]),
            ):
                if count and place != (0, 0):
                    send(
                        source(o, base + start, count), rows(o, base + start, count),
                        send_sem.at[0], fin_sem.at[INDEX[place]], to[name],
                    )
        elif kind == "c":
            if o != (0, 0):
                wait(rows(o, theirs, HALF), fin_sem.at[k])
            send(source(o, 0, ROWS), rows(o, 0, ROWS), send_sem.at[0], core_sem.at[k], to["core"])

    first = next(n for n, op in enumerate(GATHER) if op[0] == "f")
    for op in GATHER[:first]:
        gather_op(op)

    @pl.loop(0, N)
    def _(j):
        send(
            tok_hbm.at[:, pl.ds(pl.multiple_of((j * NC + 1 - c) * ROWS, ROWS), ROWS)],
            x_oth.at[j], send_sem.at[1], tok_sem.at[0], to["core"],
        )

    acc[...] = jnp.zeros_like(acc)
    groups, order = [[]], []
    for op in GATHER[first:]:
        if op[0] == "d":
            order.append((op[1], op[2]))
            groups.append([])
        else:
            groups[-1].append(op)

    @pl.loop(0, N)
    def _(t):
        dispatch(t, [functools.partial(all_of, gather_op, ops) if ops else None for ops in groups[:N]])

        @pl.when(t == 0)
        def _():
            w_load.wait()
            wait(x_own, load_sem.at[1])

        step = pick(t, [INDEX[o] * 16 + e for o, e in zip(order, encoded(order))])
        k = quo(step, 16)
        zz, xx = chip_of(rem(step, 16))
        a, b = at(zz, xx, c), at(zz, xx, 1 - c)
        rows_a = pl.ds(pl.multiple_of(a * ROWS, ROWS), ROWS)
        rows_b = pl.ds(pl.multiple_of(b * ROWS, ROWS), ROWS)
        wait(wfull.at[rows_b], core_sem.at[k])
        acc[...] += jnp.dot(x_own[a], wfull[rows_a, :], preferred_element_type=F32) + jnp.dot(
            x_own[b], wfull[rows_b, :], preferred_element_type=F32
        )

    root_width = math.sqrt(D)
    grad_scale = math.sqrt(D / (TOK * NZ * NX * NC))
    t_load.wait()
    for h in range(2):
        toks = slice(h * (TOK // 2), (h + 1) * (TOK // 2))
        cot = (acc[toks, :] * (1.0 / root_width) - tgt[toks, :].astype(F32)) * grad_scale
        cot_t = cot.T.astype(BF16)
        for j in range(NG):
            for q in range(QR):
                cot_own[h, q * PART + j * WIDTH : q * PART + (j + 1) * WIDTH, :] = cot_t[
                    j * OWN + q * WIDTH : j * OWN + (q + 1) * WIDTH
                ]
        send(cot_own.at[h], cot_par.at[h], send_sem.at[2], cot_sem.at[0], to["core"])

    w_t[...] = wfull[pl.ds(pl.multiple_of(f * ROWS, ROWS), ROWS), :].astype(F32).T
    wait(x_oth, tok_sem.at[0])
    wait(cot_par, cot_sem.at[0])

    def total(o, s, q):
        part = pl.ds(q * PART, PART)
        got = gbuf[INDEX[o], s, part, :]
        for child in children(o, s):
            kc = INDEX[child]
            wait(rbuf.at[kc, s, part], rs_sem.at[kc, s, q])
            got = got + rbuf[kc, s, part, :].astype(F32)
        return got

    def owner_part(s, q):
        part = pl.ds(q * PART, PART)
        delta = (total((0, 0), s, q) * (inner_rate / root_width)).reshape(PART // BLOCK, BLOCK, LANES)
        largest = jnp.max(jnp.abs(delta), axis=1, keepdims=True)
        block_scale = jnp.exp2(jnp.ceil(jnp.log2(largest / 6.0 + 1e-30))).astype(BF16).astype(F32)
        code = jnp.clip(delta * (1.0 / block_scale), -6.0, 6.0).astype(BF16)
        dec[s, part, :] = (code.astype(F32) * block_scale).reshape(PART, LANES).astype(BF16)
        for step in range(1, NG):
            other = rem(g + step, NG)
            send(
                dec.at[s, pl.ds(pl.multiple_of(q * PART + other * WIDTH, WIDTH), WIDTH)],
                gsum.at[s, g, pl.ds(q * WIDTH, WIDTH)], send_sem.at[4], ex_sem.at[s], {"group": other, "fsdp": f},
            )
        gsum[s, g, pl.ds(q * WIDTH, WIDTH), :] = dec[s, pl.ds(pl.multiple_of(q * PART + g * WIDTH, WIDTH), WIDTH), :]

    def sum_op(op):
        o, s, q = (op[1], op[2]), op[3], op[4]
        if o == (0, 0):
            owner_part(s, q)
            return
        k, part = INDEX[o], pl.ds(q * PART, PART)
        if children(o, s):
            sbuf[k, s, part, :] = total(o, s, q).astype(BF16)
        send(
            sbuf.at[k, s, part], rbuf.at[k, s, part],
            send_sem.at[3], rs_sem.at[k, s, q], to[REVERSE[SUM_TREE[o, s][0]]],
        )

    sum_groups, sum_order = [[]], []
    for op in SUM:
        if op[0] == "u":
            sum_order.append((op[1], op[2]))
            sum_groups.append([])
        else:
            sum_groups[-1].append(op)

    @pl.loop(0, N)
    def _(t):
        step = pick(t, [INDEX[o] * 16 + e for o, e in zip(sum_order, encoded(sum_order))])
        k = quo(step, 16)
        zz, xx = chip_of(rem(step, 16))
        x_a, x_b = x_own[at(zz, xx, c)], x_oth[zz * NX + xx]
        half = TOK // 2
        grad = jnp.dot(cot_own[0], x_a[:half], preferred_element_type=F32)
        grad += jnp.dot(cot_own[1], x_a[half:], preferred_element_type=F32)
        grad += jnp.dot(cot_par[0], x_b[:half], preferred_element_type=F32)
        grad += jnp.dot(cot_par[1], x_b[half:], preferred_element_type=F32)
        for s in range(2):
            gbuf[k, s] = grad[:, s * LANES : (s + 1) * LANES]
            sbuf[k, s] = grad[:, s * LANES : (s + 1) * LANES].astype(BF16)
        dispatch(t, [functools.partial(all_of, sum_op, ops) if ops else None for ops in sum_groups[1:N]])

    for op in sum_groups[N]:
        sum_op(op)

    m_load.wait()
    mine_rows = pl.multiple_of(g * OWN, OWN)
    tail = [op[3] for op in SUM if op[0] == "p" and (op[1], op[2]) == (0, 0)]
    turn = (1 - tail[-1], tail[-1])
    for s in turn:
        wait(gsum.at[s, pl.ds(0, NG - 1)], ex_sem.at[s])
        summed = gsum[s, 0].astype(F32)
        for step in range(1, NG):
            summed = summed + gsum[s, step].astype(F32)
        average = summed * (1.0 / NG)
        lanes = slice(s * LANES, (s + 1) * LANES)
        new_mom = momentum_decay * mom[:, lanes] + average
        own_w = w_t[pl.ds(mine_rows, OWN), lanes]
        upd[s] = (own_w - outer_rate * (average + momentum_decay * new_mom)).astype(BF16)
        for step in range(1, NG):
            send(
                upd.at[s], nw_hbm.at[pl.ds(mine_rows, OWN), pl.ds(s * LANES, LANES)], send_sem.at[5], up_sem.at[0],
                {"group": rem(g + step, NG), "fsdp": f},
            )
        pltpu.make_async_copy(
            upd.at[s], nw_hbm.at[pl.ds(mine_rows, OWN), pl.ds(s * LANES, LANES)], out_sem.at[1]
        ).start()
        nm[:, lanes] = new_mom
    nm_out = pltpu.make_async_copy(nm, nm_hbm, out_sem.at[0])
    nm_out.start()

    wait(wfull.at[pl.ds(0, (N - 1) * ROWS + N * ROWS)], send_sem.at[0])
    wait(x_oth, send_sem.at[1])
    wait(cot_own, send_sem.at[2])
    wait(sbuf.at[pl.ds(0, N - 1)], send_sem.at[3])
    wait(gsum.at[:, pl.ds(0, NG - 1)], send_sem.at[4])
    wait(gsum.at[:, pl.ds(0, NG - 1)], send_sem.at[5])
    nm_out.wait()
    wait(upd, out_sem.at[1])
    wait(gsum.at[:, pl.ds(0, NG - 1)], up_sem.at[0])


def finish(nw_t, nm_t, nw, nm):
    nw[...] = nw_t[...].astype(F32).T.astype(BF16)
    nm[...] = nm_t[...]


def body(tokens, target, weight, momentum):
    hbm = pl.BlockSpec(memory_space=pl.ANY)
    dma = pltpu.SemaphoreType.DMA
    nw_t, nm_t = pl.pallas_call(
        kernel,
        out_shape=(
            jax.ShapeDtypeStruct((KVW, ROWS), BF16),
            jax.ShapeDtypeStruct((OWN, ROWS), F32),
        ),
        in_specs=[hbm] * 4,
        out_specs=(hbm, hbm),
        scratch_shapes=[
            pltpu.VMEM((NZ * NX * NC, TOK, ROWS), BF16),
            pltpu.VMEM((N, TOK, ROWS), BF16),
            pltpu.VMEM((D, KVW), BF16),
            pltpu.VMEM((TOK, KVW), F32),
            pltpu.VMEM((TOK, KVW), BF16),
            pltpu.VMEM((OWN, ROWS), F32),
            pltpu.VMEM((2, KVW, TOK // 2), BF16),
            pltpu.VMEM((2, KVW, TOK // 2), BF16),
            pltpu.VMEM((N, 2, KVW, LANES), F32),
            pltpu.VMEM((N, 2, KVW, LANES), BF16),
            pltpu.VMEM((N, 2, KVW, LANES), BF16),
            pltpu.VMEM((2, KVW, LANES), BF16),
            pltpu.VMEM((2, NG, OWN, LANES), BF16),
            pltpu.VMEM((KVW, ROWS), F32),
            pltpu.VMEM((2, OWN, LANES), BF16),
            pltpu.VMEM((OWN, ROWS), F32),
            dma((4,)), dma((2,)), dma((6,)), dma((N, 2, QG)), dma((N,)), dma((N,)), dma((1,)), dma((1,)),
            dma((N, 2, QR)), dma((2,)), dma((1,)),
        ],
        compiler_params=pltpu.CompilerParams(
            collective_id=0, has_side_effects=True, vmem_limit_bytes=56 * 1024 * 1024
        ),
        cost_estimate=pl.CostEstimate(
            flops=4 * TOK * D * KVW, bytes_accessed=2 * TOK * D + 4 * ROWS * KVW, transcendentals=0
        ),
    )(tokens, target, weight, momentum.T)
    new_weight, new_momentum_t = pl.pallas_call(
        finish,
        out_shape=(
            jax.ShapeDtypeStruct((ROWS, KVW), BF16),
            jax.ShapeDtypeStruct((OWN, ROWS), F32),
        ),
    )(nw_t, nm_t)
    return (new_weight, new_momentum_t.T)


def solution(mesh):
    placed = (
        P(("group", "fsdp"), None),
        P(("group", "fsdp"), None),
        P("fsdp", None),
        P("fsdp", "group"),
    )
    return jax.shard_map(
        body,
        mesh=mesh,
        in_specs=placed,
        out_specs=(P("fsdp", None), P("fsdp", "group")),
        check_vma=False,
    )
```
